256 devices in a mesh: dp: 16 (over x, y), seq: 16 (over z, core).
Axes of the slice: x: 4, y: 4, z: 8, core: 2. Of those that a mesh axis runs over, the one named last changes fastest.
Arguments:
- features: bfloat16 [128, 32, 32, 512], P('dp', 'seq'), may hold values from -6 to 6
- conv_weight: bfloat16 [3, 3, 3, 16, 512], replicated, may hold values from -0.0546875 to 0.0546875
- clip_frames: int32 [32], replicated, may hold values from 1 to 7, as said below
- clip_group: int32 [32], replicated, may hold values from 0 to 15, as said below
- clip_offset: int32 [32], replicated, may hold values from 0 to 7, as said below
- clip_times: float32 [32], replicated, may hold values from 0.05 to 0.95
- noise_tokens: bfloat16 [16, 2048, 64], P('dp', 'seq'), may hold values from -6 to 6
- embed_weight: bfloat16 [64, 2048], replicated, may hold values from -0.75 to 0.75
- attention_proj: bfloat16 [2048, 3, 16, 128], P(None, None, 'seq'), may hold values from -0.125 to 0.125
- norm_gains: float32 [2, 128], replicated, may hold values from 0.5 to 1.5
- cotangent: bfloat16 [16, 2048, 2048], P('dp', 'seq'), may hold values from -0.03125 to 0.03125
Outputs:
- noisy_tokens: float32 [16, 2048, 64], P('dp', 'seq')
- attention_out: bfloat16 [16, 2048, 2048], P('dp', 'seq')
- proj_grad: float32 [2048, 3, 16, 128], P('dp', None, 'seq')
- norm_grad: float32 [2, 128], replicated
The draws below stay inside these ranges and needn't reach their ends.
Inputs may be any that keep to these rules, and one draw needn't show every extreme that they name: `clip_frames`: clips follow one another along time from frame 0 and together cover all 128 frames. `clip_group`: every group trains on exactly two clips, whose frames add up to 8. `clip_offset`: the clips of one group take consecutive frame slots from slot 0 in their time order and fill all 8 slots of the group.
All inputs are finite; a program needn't handle non-finite values.
Results may differ from the reference program's by a relative error of at most 0.014.
Values may be sent and summed in bfloat16 or wider, within the bound.
A program may use at most 128 MiB of HBM per device.

```python
import jax
import jax.numpy as jnp
from jax import lax

D = 2048
HEAD_DIM = 128
CIN = 512
LAT = 16
WD = 32
FR_DEV = 8
HEADS = 16
HT = 32
TPR = 16
TOK_DEV = 128
SEQLEN = 2048
FRAMES = 128
CLIPS = 32
N_DP = 16
N_SEQ = 16


def clip_plan(key):
    base_key = jax.random.fold_in(key, 11)
    key_order, key_sizes = jax.random.split(base_key, 2)
    group_count = CLIPS // 2
    order = jax.random.permutation(key_order, group_count).astype(jnp.int32)
    owners = jnp.concatenate([order, order]).astype(jnp.int32)
    first_len = jax.random.randint(key_sizes, (group_count,), 1, FR_DEV).astype(jnp.int32)
    positions = jnp.arange(group_count).astype(jnp.int32)
    first_len = jnp.where(positions == 0, FR_DEV - 1, jnp.where(positions == group_count - 1, 1, first_len)).astype(jnp.int32)
    lengths = jnp.concatenate([first_len, FR_DEV - first_len]).astype(jnp.int32)
    offsets = jnp.concatenate([jnp.zeros((group_count,), jnp.int32), first_len]).astype(jnp.int32)
    return (lengths, owners, offsets)


def draw_clip_frames(key, part):
    return clip_plan(key)[0]


def draw_clip_group(key, part):
    return clip_plan(key)[1]


def draw_clip_offset(key, part):
    return clip_plan(key)[2]


def block_scale(rng, dims, cuts, low, largest):
    def one(axis_at, parts):
        heights = jax.random.uniform(jax.random.fold_in(jax.random.fold_in(rng, 6), axis_at), (parts,), jnp.float32, low / len(cuts), largest / len(cuts))
        return jnp.repeat(jnp.exp(heights), dims[axis_at] // parts).reshape((-1,) + (1,) * (len(dims) - axis_at - 1))

    level = one(*cuts[0])
    for cut in cuts[1:]:
        level = level * one(*cut)
    return level


def centred(own_key, extent, width, limit, pieces=(), kind=jnp.bfloat16):
    drawn = width * jax.random.normal(own_key, extent, jnp.float32)
    if pieces:
        drawn = drawn * block_scale(own_key, extent, pieces, -0.22, 0.18)
    return jnp.clip(drawn, -limit, limit).astype(kind)


def setup_inputs(seed: int = 0) -> dict:
    splits = jax.random.split(jax.random.key(seed), 12)
    features = centred(splits[0], (FRAMES, HT, WD, CIN), 1.0, 6.0, ((0, 16), (1, 16)))
    conv_weight = centred(splits[1], (3, 3, 3, LAT, CIN), (27 * CIN) ** -0.5, 0.0546875)
    clip_frames = draw_clip_frames(jax.random.fold_in(splits[11], 71), 0)
    clip_group = draw_clip_group(jax.random.fold_in(splits[11], 71), 0)
    clip_offset = draw_clip_offset(jax.random.fold_in(splits[11], 71), 0)
    clip_times = jnp.clip(jax.random.uniform(splits[5], (CLIPS,), jnp.float32, 0.05, 0.95), 0.05, 0.95)
    noise_tokens = centred(splits[6], (N_DP, SEQLEN, 4 * LAT), 1.0, 6.0, ((0, 16), (1, 16)))
    embed_weight = centred(splits[7], (4 * LAT, D), (4 * LAT) ** -0.5, 0.75)
    attention_proj = centred(splits[8], (D, 3, HEADS, HEAD_DIM), D ** -0.5, 0.125, ((2, 16),))
    norm_gains = jnp.clip(1.0 + 0.1 * jax.random.normal(splits[9], (2, HEAD_DIM), jnp.float32), 0.5, 1.5)
    cotangent = centred(splits[10], (N_DP, SEQLEN, HEADS * HEAD_DIM), (1.0 / (N_DP * SEQLEN) ** 0.5), 0.03125, ((0, 16), (1, 16)))
    return {"features": features, "conv_weight": conv_weight, "clip_frames": clip_frames, "clip_group": clip_group, "clip_offset": clip_offset, "clip_times": clip_times, "noise_tokens": noise_tokens, "embed_weight": embed_weight, "attention_proj": attention_proj, "norm_gains": norm_gains, "cotangent": cotangent}


def clip_bounds(clip_frames):
    ends_at = jnp.cumsum(clip_frames).astype(jnp.int32)
    return ((ends_at - clip_frames).astype(jnp.int32), ends_at)

def frame_start(frame_ids, starts_at, ends_at):
    member = (frame_ids[:, None] >= starts_at[None, :]) & (frame_ids[:, None] < ends_at[None, :])
    own_start = lax.optimization_barrier(jnp.sum(jnp.where(member, starts_at[None, :], 0), axis=1)).astype(jnp.int32)
    return (own_start, member)

def slot_table(group_id, slot_ids, clip_group, clip_offset, clip_frames, starts_at, clip_times):
    member = (clip_group[None, :] == group_id) & (slot_ids[:, None] >= clip_offset[None, :]) & (slot_ids[:, None] < clip_offset[None, :] + clip_frames[None, :])
    numbers = jnp.arange(clip_frames.shape[0]).astype(jnp.int32)
    usable = jnp.any(member, axis=1).astype(jnp.float32)
    segment = (lax.optimization_barrier(jnp.sum(jnp.where(member, numbers[None, :] + 1, 0), axis=1)) - 1).astype(jnp.int32)
    source = lax.optimization_barrier(jnp.sum(jnp.where(member, starts_at[None, :] + slot_ids[:, None] - clip_offset[None, :], 0), axis=1)).astype(jnp.int32)
    noise_level = lax.optimization_barrier(jnp.sum(jnp.where(member, clip_times[None, :], jnp.zeros((), clip_times.dtype)), axis=1))
    return (usable, segment, source, noise_level)

def rms_scale(values, gain_row):
    inverse = lax.rsqrt(lax.optimization_barrier(jnp.mean(values * values, axis=-1, keepdims=True)) + 1e-06)
    return (values * inverse * gain_row, inverse)

def rms_back(values, inverse, gain_row, upstream):
    scaled = gain_row * upstream
    grad_in = inverse * scaled - values * inverse ** 3 * lax.optimization_barrier(jnp.mean(values * scaled, axis=-1, keepdims=True))
    gain_part = lax.optimization_barrier(jnp.sum(upstream * values * inverse, axis=(0, 1)))
    return (grad_in, gain_part)

def head_pass(operands):
    queries, key_rows, value_rows, grad_rows, segment_ids = operands
    score_scale = HEAD_DIM ** (-0.5)
    same_clip = segment_ids[:, None] == segment_ids[None, :]
    scores = jnp.dot(queries, key_rows.T, preferred_element_type=jnp.float32) * score_scale
    exp_scores = jnp.where(same_clip, jnp.exp(scores), 0.0)
    prob_rows = exp_scores / lax.optimization_barrier(jnp.sum(exp_scores, axis=1, keepdims=True))
    probs_bf = prob_rows.astype(jnp.bfloat16)
    output = jnp.dot(probs_bf, value_rows, preferred_element_type=jnp.float32)
    prob_grad = jnp.dot(grad_rows, value_rows.T, preferred_element_type=jnp.float32)
    row_delta = lax.optimization_barrier(jnp.sum(prob_rows * prob_grad, axis=1, keepdims=True))
    score_grad = (prob_rows * (prob_grad - row_delta) * score_scale).astype(jnp.bfloat16)
    query_grad = jnp.dot(score_grad, key_rows, preferred_element_type=jnp.float32)
    key_grad = jnp.dot(score_grad.T, queries, preferred_element_type=jnp.float32)
    value_grad = jnp.dot(probs_bf.T, grad_rows, preferred_element_type=jnp.float32)
    return (output, query_grad, key_grad, value_grad)

def reference(features, conv_weight, clip_frames, clip_group, clip_offset, clip_times, noise_tokens, embed_weight, attention_proj, norm_gains, cotangent):
    starts_at, ends_at = clip_bounds(clip_frames)
    frame_ids = jnp.arange(FRAMES).astype(jnp.int32)
    own_start, member = frame_start(frame_ids, starts_at, ends_at)
    activated = jax.nn.silu(features.astype(jnp.float32)).astype(jnp.bfloat16)
    padded = jnp.pad(activated, ((2, 0), (1, 1), (1, 1), (0, 0)))
    latent = jnp.zeros((FRAMES * HT * WD, LAT), jnp.float32)
    for tap_time in range(3):
        allowed = (frame_ids - (2 - tap_time) >= own_start).astype(jnp.float32)
        allowed_rows = jnp.repeat(allowed, HT * WD)[:, None]
        for tap_row in range(3):
            for tap_col in range(3):
                tap_piece = padded[tap_time:tap_time + FRAMES, tap_row:tap_row + HT, tap_col:tap_col + WD].reshape(-1, CIN)
                tap_term = jnp.dot(tap_piece, conv_weight[tap_time, tap_row, tap_col].T, preferred_element_type=jnp.float32)
                latent = latent + allowed_rows * tap_term
    patches = latent.reshape(FRAMES, N_SEQ, 2, TPR, 2, LAT).transpose(0, 1, 3, 2, 4, 5).reshape(FRAMES, N_SEQ, TPR, 4 * LAT)
    slot_ids = jnp.arange(FR_DEV).astype(jnp.int32)
    group_ids = jnp.arange(N_DP).astype(jnp.int32)
    usable, segment, source, noise_level = jax.vmap(slot_table, in_axes=(0, None, None, None, None, None, None))(group_ids, slot_ids, clip_group, clip_offset, clip_frames, starts_at, clip_times)
    picked = patches[source].transpose(0, 2, 1, 3, 4).reshape(N_DP, SEQLEN, 4 * LAT)
    slot_of_token = (jnp.arange(SEQLEN) % TOK_DEV // TPR).astype(jnp.int32)
    tok_usable = usable[:, slot_of_token]
    tok_level = noise_level[:, slot_of_token]
    tok_segment = segment[:, slot_of_token]
    noisy_tokens = tok_usable[..., None] * ((1.0 - tok_level[..., None]) * picked + tok_level[..., None] * noise_tokens.astype(jnp.float32))
    proj_flat = attention_proj.reshape(D, 3 * HEADS * HEAD_DIM)

    def group_step(running, inputs):
        proj_acc, gain_acc = running
        tokens_group, usable_group, segment_group, cot_group = inputs
        hidden = jnp.dot(tokens_group.astype(jnp.bfloat16), embed_weight, preferred_element_type=jnp.float32).astype(jnp.bfloat16)
        mixed_all = jnp.dot(hidden, proj_flat, preferred_element_type=jnp.float32).reshape(SEQLEN, 3, HEADS, HEAD_DIM)
        query_n, query_inv = rms_scale(mixed_all[:, 0], norm_gains[0])
        key_n, key_inv = rms_scale(mixed_all[:, 1], norm_gains[1])
        query_bf = query_n.astype(jnp.bfloat16)
        key_bf = key_n.astype(jnp.bfloat16)
        value_bf = mixed_all[:, 2].astype(jnp.bfloat16)
        incoming = jnp.where(usable_group[:, None, None] > 0, cot_group.reshape(SEQLEN, HEADS, HEAD_DIM), jnp.zeros((), jnp.bfloat16))
        segments_h = jnp.broadcast_to(segment_group[None, :], (HEADS, SEQLEN))
        output, query_grad, key_grad, value_grad = lax.map(head_pass, (query_bf.transpose(1, 0, 2), key_bf.transpose(1, 0, 2), value_bf.transpose(1, 0, 2), incoming.transpose(1, 0, 2), segments_h))
        attention_group = (usable_group[:, None, None] * output.transpose(1, 0, 2)).astype(jnp.bfloat16).reshape(SEQLEN, HEADS * HEAD_DIM)
        query_in, query_gain = rms_back(mixed_all[:, 0], query_inv, norm_gains[0], query_grad.transpose(1, 0, 2))
        key_in, key_gain = rms_back(mixed_all[:, 1], key_inv, norm_gains[1], key_grad.transpose(1, 0, 2))
        stacked = jnp.stack([query_in, key_in, value_grad.transpose(1, 0, 2)], axis=1).astype(jnp.bfloat16).reshape(SEQLEN, 3 * HEADS * HEAD_DIM)
        proj_term = lax.dot_general(hidden, stacked, (((0,), (0,)), ((), ())), preferred_element_type=jnp.float32)
        return ((proj_acc + proj_term, gain_acc + jnp.stack([query_gain, key_gain])), attention_group)
    start_state = (jnp.zeros((D, 3 * HEADS * HEAD_DIM), jnp.float32), jnp.zeros((2, HEAD_DIM), jnp.float32))
    final_state, attention_out = lax.scan(group_step, start_state, (noisy_tokens, tok_usable, tok_segment, cotangent))
    proj_grad = final_state[0].reshape(D, 3, HEADS, HEAD_DIM)
    return (noisy_tokens, attention_out, proj_grad, final_state[1])
```

```python
import jax
import jax.numpy as jnp
from jax import lax
from jax.experimental import pallas as pl
from jax.experimental.pallas import tpu as pltpu
from jax.sharding import PartitionSpec as P

F32 = jnp.float32
BF = jnp.bfloat16
N = 16
LN2 = 0.6931471805599453
MASKED = -300.0
EPS = 1e-06


def nn(a, b):
    return lax.dot_general(a, b, (((1,), (0,)), ((), ())), preferred_element_type=F32)


def nt(a, b):
    return lax.dot_general(a, b, (((1,), (1,)), ((), ())), preferred_element_type=F32)


def iota(shape, dim):
    return lax.broadcasted_iota(jnp.int32, shape, dim)


def block_of(i, size=128):
    return pl.ds(pl.multiple_of(i * size, size), size)


def peer(axis, k):
    return lax.rem(lax.axis_index(axis) + k + N, N)


def greet(axes):
    barrier = pltpu.get_barrier_semaphore()

    def signal(k, _):
        for axis in axes:
            pl.semaphore_signal(
                barrier, inc=1, device_id={axis: peer(axis, k)}, device_id_type=pl.DeviceIdType.MESH
            )
        return 0

    lax.fori_loop(1, N, signal, 0)
    return lambda: pl.semaphore_wait(barrier, (N - 1) * len(axes))


def remote(src, dst, send, recv, axis, where):
    return pltpu.make_async_remote_copy(
        src_ref=src,
        dst_ref=dst,
        send_sem=send,
        recv_sem=recv,
        device_id={axis: where},
        device_id_type=pl.DeviceIdType.MESH,
    )


def to_all(make):
    def start(k, _):
        make(k).start()
        return 0

    def wait(k, _):
        make(k).wait()
        return 0

    lax.fori_loop(1, N, start, 0)
    return lambda: lax.fori_loop(1, N, wait, 0)


def split(x):
    high = x.astype(BF)
    return high, (x - high.astype(F32)).astype(BF)


def front(
    feat, wconv, tab, noise, embed, proj, cot,
    noisy, tokens, incoming, ew_kv, ew_q, slots,
    actf, actp, conv, edge_out, edge_in, gath,
    edge_send, edge_recv, dp_send, dp_recv, seq_send, seq_recv, cot_send, cot_recv, own_sem,
):
    slab = lax.axis_index("dp")
    row = lax.axis_index("seq")
    entered = greet(("dp", "seq"))

    for q in range(4):
        x = feat[:, q * 128 : q * 128 + 128].astype(F32)
        actf[q] = x / (1.0 + jnp.exp(-x))
    entered()

    own = pltpu.make_async_copy(cot.at[:, block_of(row)], incoming.at[block_of(row)], own_sem)
    own.start()
    cot_wait = to_all(
        lambda k: remote(
            cot.at[:, block_of(peer("seq", k))], incoming.at[block_of(row)],
            cot_send.at[k], cot_recv.at[k], "seq", peer("seq", k),
        )
    )

    for part in range(4):
        r, b = part // 2, part % 2
        for t in range(8):
            for q in range(4):
                rows = actf[q, pl.ds(t * 64 + r * 32 + b, 16, stride=2), :]
                actp[pl.ds((part * 8 + t) * 16, 16), q * 128 : q * 128 + 128] = rows.astype(BF)
    conv[...] = nt(wconv[...], actp[...])

    by_clip = tab[...].T
    frames, group, offset, times = [by_clip[0:32, i : i + 1] for i in range(4)]
    earlier = iota((32, 128), 1) < iota((32, 128), 0)
    starts = jnp.sum(jnp.where(earlier, tab[0:1, :], 0.0), axis=1, keepdims=True)
    lane = iota((1, 128), 1)
    slot_i = lax.shift_right_logical(lane, 4)
    col_i = lax.bitwise_and(lane, 15)
    slot = slot_i.astype(F32)
    in_slot = (group == slab.astype(F32)) & (slot >= offset) & (slot < offset + frames)
    over_clips = lambda v: jnp.sum(jnp.where(in_slot, v, 0.0), axis=0, keepdims=True)
    number = iota((32, 128), 0).astype(F32)
    usable = over_clips(1.0 + 0.0 * number)
    usable = jnp.where(usable > 0.0, 1.0, 0.0)
    segment = over_clips(number + 1.0) - 1.0
    source = over_clips(starts + slot - offset)
    level = over_clips(times + 0.0 * number)
    slots[0:1, :] = segment
    slots[1:2, :] = usable
    slots[2:8, :] = jnp.zeros((6, 128), F32)

    def own_start(frame):
        inside = (starts <= frame) & (frame < starts + frames)
        return jnp.sum(jnp.where(inside, starts, 0.0), axis=0, keepdims=True)

    here = slab.astype(F32) * 8.0 + slot
    after = here + 8.0
    start_here, start_after = own_start(here), own_start(after)
    keep = []
    for dt in range(3):
        main = (here - dt >= start_here) & (slot_i >= dt)
        late = (after - dt >= start_after) & (slot_i < dt)
        keep.append((jnp.where(main, 1.0, 0.0), jnp.where(late, 1.0, 0.0)))

    not_first = jnp.where(col_i > 0, 1.0, 0.0)
    not_last = jnp.where(col_i < 15, 1.0, 0.0)

    def tap(dt, dr, dw, r, ob):
        at = (((2 - dt) * 3 + dr + 1) * 3 + dw + 1) * 16
        b = (ob + dw) % 2
        piece = conv[at : at + 16, (r * 2 + b) * 128 : (r * 2 + b) * 128 + 128]
        if ob + dw == -1:
            return pltpu.roll(piece, 1, 1) * not_first
        if ob + dw == 2:
            return pltpu.roll(piece, 127, 1) * not_last
        return piece

    mains, lates = {}, {}
    for out_row in range(-1, 3):
        for ob in range(2):
            main = late = None
            for dt in range(3):
                total = None
                for r in range(2):
                    dr = r - out_row
                    if abs(dr) <= 1:
                        for dw in range(-1, 2):
                            term = tap(dt, dr, dw, r, ob)
                            total = term if total is None else total + term
                if dt:
                    total = pltpu.roll(total, 16 * dt, 1)
                m = total * keep[dt][0]
                main = m if main is None else main + m
                if dt:
                    m = total * keep[dt][1]
                    late = m if late is None else late + m
            mains[out_row, ob], lates[out_row, ob] = main, late
    for side, out_row in ((0, -1), (1, 2)):
        for ob in range(2):
            edge_out[side, ob * 16 : ob * 16 + 16, :] = mains[out_row, ob]
            edge_out[side, 32 + ob * 16 : 48 + ob * 16, :] = lates[out_row, ob]

    up = remote(edge_out.at[0], edge_in.at[1], edge_send.at[0], edge_recv.at[1], "seq", peer("seq", -1))
    down = remote(edge_out.at[1], edge_in.at[0], edge_send.at[1], edge_recv.at[0], "seq", peer("seq", 1))

    @pl.when(row > 0)
    def _():
        up.start()

    @pl.when(row < N - 1)
    def _():
        down.start()

    @pl.when(row == 0)
    def _():
        edge_in[0] = jnp.zeros((64, 128), F32)

    @pl.when(row == N - 1)
    def _():
        edge_in[1] = jnp.zeros((64, 128), F32)

    for j in range(3):
        high, low = split(nn(embed[...], proj[j]))
        if j == 0:
            both = jnp.concatenate([high.astype(F32), low.astype(F32)], axis=0)
            ew_q[...] = both.T.astype(BF)
        else:
            ew_kv[0:64, (j - 1) * 128 : j * 128] = high
            ew_kv[64:128, (j - 1) * 128 : j * 128] = low

    @pl.when(row > 0)
    def _():
        up.wait_send()
        down.wait_recv()

    @pl.when(row < N - 1)
    def _():
        down.wait_send()
        up.wait_recv()

    packed = jnp.zeros((16, 128), F32)
    for a in range(2):
        for ob in range(2):
            ab = a * 2 + ob
            main = mains[a, ob] + edge_in[a, ob * 16 : ob * 16 + 16, :]
            late = lates[a, ob] + edge_in[a, 32 + ob * 16 : 48 + ob * 16, :]
            gath[ab * 16 : ab * 16 + 16, block_of(slab)] = main.astype(BF)
            packed = packed + (pltpu.roll(late, 32 * ab, 1) if ab else late)
    gath[64:80, block_of(slab)] = packed.astype(BF)
    mine = gath.at[:, block_of(slab)]
    gath_wait = to_all(
        lambda k: remote(mine, mine, dp_send.at[k], dp_recv.at[k], "dp", peer("dp", k))
    )

    base = source * 16.0 + col_i.astype(F32)
    k_i = iota((2048, 128), 0)
    select = jnp.where(k_i.astype(F32) == base, 1.0, 0.0).astype(BF)
    slab_of = jnp.floor(source * 0.125)
    inner = source - slab_of * 8.0
    crosses = (inner < 2.0) & (slab_of >= 1.0)
    late_at = jnp.where(crosses, (slab_of - 1.0) * 32.0 + inner * 16.0 + col_i.astype(F32), -1.0)
    k_late = lax.shift_right_logical(k_i, 7) * 32 + lax.bitwise_and(k_i, 31)
    select_late = jnp.where(k_late.astype(F32) == late_at, 1.0, 0.0).astype(BF)
    gath_wait()

    wide = lax.bitwise_and(lax.shift_right_logical(iota((16, 2048), 1), 5), 3)
    lates_all = gath[64:80, :].astype(F32)
    spread = jnp.concatenate([jnp.where(wide == ab, lates_all, 0.0) for ab in range(4)], axis=0)
    picked = nn(gath[0:64, :], select) + nn(spread.astype(BF), select_late)
    made = usable * ((1.0 - level) * picked + level * noise[...].astype(F32))
    noisy[...] = made
    tokens[:, block_of(row)] = made.astype(BF)
    tile = tokens.at[:, block_of(row)]
    token_wait = to_all(
        lambda k: remote(tile, tile, seq_send.at[k], seq_recv.at[k], "seq", peer("seq", k))
    )
    token_wait()
    cot_wait()
    own.wait()


def attention(
    tokens, ew_kv, ew_q, incoming, slots, gains, embed,
    att, proj_out, norm_out,
    two, keys, vals, keys_t, vals_t, xk, dk, dv, exps, qx, gx, dxq, dkv, nq, outs,
    parts, landed, sums, norms,
    att_send, att_recv, own_sem, rs_send, rs_recv, nrm_send, nrm_recv, ag_send, ag_recv,
):
    slab = lax.axis_index("dp")
    head = lax.axis_index("seq")
    entered = greet(("dp", "seq"))
    scale = 128.0**-0.5
    gain_k = gains[1:2, :]
    gain_q = gains[...].T[:, 0:1]
    seg_row, use_row = slots[0:1, :], slots[1:2, :]
    seg_col = slots[...].T[:, 0:1]
    class_l = iota((128, 128), 1).astype(F32) - 1.0
    class_s = iota((128, 128), 0).astype(F32) - 1.0
    key_mask = jnp.where(class_l == seg_col, 0.0, MASKED).astype(BF)
    query_mask = jnp.where(class_s == seg_row, 1.0, 0.0).astype(BF)
    ones_two = jnp.where(iota((256, 128), 1) < 2, 1.0, 0.0).astype(BF)
    use_q = jnp.concatenate([use_row, use_row], axis=1)

    qx[128:256, 0:128] = query_mask
    qx[128:256, 128:256] = query_mask
    gx[128:256, :] = jnp.zeros((128, 256), BF)
    vals_t[128:144, :] = jnp.ones((16, 2048), BF)
    dk[...] = jnp.zeros((2048, 128), F32)
    dv[...] = jnp.zeros((2048, 128), F32)
    nq[...] = jnp.zeros((128, 256), F32)

    def prepare(i, _):
        at = block_of(i, 256)
        piece = tokens[:, at].astype(F32)
        tile = jnp.concatenate([piece, piece], axis=0).T.astype(BF)
        two[at, :] = tile
        kv = nn(tile, ew_kv[...])
        x = kv[:, 0:128]
        xk[at, :] = x
        r = lax.rsqrt(jnp.mean(x * x, axis=1, keepdims=True) + EPS)
        key = x * r * gain_k
        keys[at, 0:128] = key.astype(BF)
        keys[at, 128:256] = jnp.concatenate([key_mask, key_mask], axis=0)
        keys_t[:, at] = key.T.astype(BF)
        val = kv[:, 128:256]
        vals[at, 0:128] = val.astype(BF)
        vals[at, 128:256] = ones_two
        vals_t[0:128, at] = val.T.astype(BF)
        return 0

    lax.fori_loop(0, 8, prepare, 0)
    entered()

    def send_out(p):
        return remote(
            outs.at[block_of(p)], att.at[:, block_of(head)], att_send.at[p], att_recv.at[head], "seq", p
        )

    def own_out():
        return pltpu.make_async_copy(outs.at[block_of(head)], att.at[:, block_of(head)], own_sem)

    def query_block(i, _):
        qb = lax.rem(lax.div(head, 2) + i, 8)
        at = block_of(qb, 256)
        tile = two[at, :]
        x = nt(ew_q[...], tile)
        r = lax.rsqrt(jnp.mean(x * x, axis=0, keepdims=True) + EPS)
        query = (x * (r * (scale / LN2)) * gain_q).astype(BF)
        qx[0:128, :] = query
        out = jnp.zeros((144, 256), F32)
        for c in range(4):
            kc = pl.ds(c * 512, 512)
            e = jnp.exp2(nn(keys[kc, :], qx[...])).astype(BF)
            exps[kc, :] = e
            out = out + nn(vals_t[:, kc], e)
        inverse = 1.0 / out[128:129, :]
        out = out[0:128, :] * inverse
        outs[at, :] = (out * use_q).T.astype(BF)
        for p in (qb * 2, qb * 2 + 1):
            @pl.when(p != head)
            def _():
                send_out(p).start()

            @pl.when(p == head)
            def _():
                own_out().start()

        up = jnp.where(use_q > 0.0, incoming[at, :].astype(F32).T, 0.0)
        up = (up * inverse).astype(BF)
        delta = jnp.sum(up.astype(F32) * out, axis=0, keepdims=True)
        high, low = split(-delta)
        line = iota((16, 256), 0)
        extra = jnp.where(line == 0, high.astype(F32), jnp.where(line == 1, low.astype(F32), 0.0))
        gx[0:128, :] = up
        gx[128:144, :] = extra.astype(BF)
        dq = jnp.zeros((128, 256), F32)
        for c in range(4):
            kc = pl.ds(c * 512, 512)
            e = exps[kc, :]
            ds = (e.astype(F32) * nn(vals[kc, :], gx[...])).astype(BF)
            dv[kc, :] = dv[kc, :] + nt(e, up)
            dk[kc, :] = dk[kc, :] + nt(ds, query)
            dq = dq + nn(keys_t[:, kc], ds)
        dq = dq * scale
        nq[...] = nq[...] + dq * x * r
        scaled = gain_q * dq
        mean = jnp.mean(x * scaled, axis=0, keepdims=True)
        dxq[:, at] = (r * scaled - x * (r * r * r * mean)).astype(BF)
        return 0

    lax.fori_loop(0, 8, query_block, 0)

    def key_back(i, total):
        at = block_of(i, 256)
        x = xk[at, :]
        r = lax.rsqrt(jnp.mean(x * x, axis=1, keepdims=True) + EPS)
        grad = dk[at, :] * LN2
        scaled = gain_k * grad
        mean = jnp.mean(x * scaled, axis=1, keepdims=True)
        dkv[at, 0:128] = (r * scaled - x * (r * r * r * mean)).astype(BF)
        dkv[at, 128:256] = dv[at, :].astype(BF)
        return total + jnp.sum(grad * x * r, axis=0, keepdims=True)

    norm_k = lax.fori_loop(0, 8, key_back, jnp.zeros((1, 128), F32))
    norm_q = jnp.sum(nq[...], axis=1, keepdims=True)
    norm_q = jnp.broadcast_to(norm_q, (128, 128)).T[0:1, :]
    line = iota((8, 128), 0)
    norms[head] = jnp.where(line == 0, norm_q, jnp.where(line == 1, norm_k, 0.0))
    norm_wait = to_all(
        lambda k: remote(
            norms.at[head], norms.at[head], nrm_send.at[k], nrm_recv.at[k], "seq", peer("seq", k)
        )
    )
    part_q = nn(dxq[...], two[...]).T
    part_kv = nn(tokens[...], dkv[...])
    for b in range(8):
        rows = slice(b * 8, b * 8 + 8)
        parts[2 * b, :, 0:128] = part_q[rows, :]
        parts[2 * b, :, 128:256] = part_kv[rows, 0:128]
        parts[2 * b + 1, :, 0:128] = part_kv[rows, 128:256]
        parts[2 * b + 1, :, 128:256] = jnp.zeros((8, 128), F32)
    landed[slab] = parts[slab]
    rs_wait = to_all(
        lambda k: remote(
            parts.at[peer("dp", k)], landed.at[slab], rs_send.at[k], rs_recv.at[k], "dp", peer("dp", k)
        )
    )
    columns = embed[:, block_of(slab)].astype(F32).T.astype(BF)
    norm_wait()
    rs_wait()
    total, norm = landed[0], norms[0]
    for j in range(1, N):
        total, norm = total + landed[j], norm + norms[j]
    sums[slab, 0:8, :] = total
    sums[slab, 8:16, 0:128] = norm
    sums[slab, 8:16, 128:256] = jnp.zeros((8, 128), F32)
    ag_wait = to_all(
        lambda k: remote(
            sums.at[slab], sums.at[slab], ag_send.at[k], ag_recv.at[k], "dp", peer("dp", k)
        )
    )
    ag_wait()
    even = jnp.concatenate([sums[2 * b, 0:8, :] for b in range(8)], axis=0)
    odd = jnp.concatenate([sums[2 * b + 1, 0:8, 0:128] for b in range(8)], axis=0)
    norm = sums[0, 8:16, 0:128]
    for j in range(1, N):
        norm = norm + sums[j, 8:16, 0:128]
    norm_out[...] = norm
    whole = jnp.concatenate([even, odd], axis=1)
    high, low = split(whole)
    grads = nn(columns, high) + nn(columns, low)
    for j in range(3):
        proj_out[pl.ds(j, 128, stride=3), :] = grads[:, j * 128 : j * 128 + 128]

    def out_wait(p, _):
        @pl.when(p != head)
        def _():
            send_out(p).wait_send()
            remote(
                outs.at[block_of(p)], att.at[:, block_of(p)], att_send.at[p], att_recv.at[p], "seq", p
            ).wait_recv()

        return 0

    lax.fori_loop(0, N, out_wait, 0)
    own_out().wait()


def body(
    features,
    conv_weight,
    clip_frames,
    clip_group,
    clip_offset,
    clip_times,
    noise_tokens,
    embed_weight,
    attention_proj,
    norm_gains,
    cotangent,
):
    vmem = pl.BlockSpec(memory_space=pltpu.VMEM)
    tab = jnp.stack([clip_frames.astype(F32), clip_group.astype(F32), clip_offset.astype(F32), clip_times])
    tab = jnp.pad(tab, ((0, 4), (0, 96)))
    dma = pltpu.SemaphoreType.DMA
    shape = jax.ShapeDtypeStruct
    noisy, tokens, incoming, ew_kv, ew_q, slots = pl.pallas_call(
        front,
        name="front",
        out_shape=(
            shape((64, 128), F32),
            shape((64, 2048), BF),
            shape((2048, 128), BF),
            shape((128, 256), BF),
            shape((128, 128), BF),
            shape((8, 128), F32),
        ),
        in_specs=[vmem] * 7,
        out_specs=[vmem] * 6,
        scratch_shapes=[
            pltpu.VMEM((4, 512, 128), F32),
            pltpu.VMEM((512, 512), BF),
            pltpu.VMEM((432, 512), F32),
            pltpu.VMEM((2, 64, 128), F32),
            pltpu.VMEM((2, 64, 128), F32),
            pltpu.VMEM((80, 2048), BF),
            dma((2,)),
            dma((2,)),
            dma((N,)),
            dma((N,)),
            dma((N,)),
            dma((N,)),
            dma((N,)),
            dma((N,)),
            dma,
        ],
        compiler_params=pltpu.CompilerParams(
            collective_id=0, has_side_effects=True, vmem_limit_bytes=40 * 2**20
        ),
    )(
        features.reshape(512, 512),
        conv_weight.reshape(432, 512),
        tab,
        noise_tokens.transpose(0, 2, 1).reshape(64, 128),
        embed_weight,
        attention_proj.transpose(1, 2, 0, 3).reshape(3, 2048, 128),
        cotangent.reshape(128, 2048),
    )
    att, grads, norms = pl.pallas_call(
        attention,
        name="attention",
        out_shape=(shape((128, 2048), BF), shape((384, 128), F32), shape((8, 128), F32)),
        in_specs=[vmem] * 7,
        out_specs=[vmem] * 3,
        scratch_shapes=[
            pltpu.VMEM((2048, 128), BF),
            pltpu.VMEM((2048, 256), BF),
            pltpu.VMEM((2048, 256), BF),
            pltpu.VMEM((128, 2048), BF),
            pltpu.VMEM((144, 2048), BF),
            pltpu.VMEM((2048, 128), F32),
            pltpu.VMEM((2048, 128), F32),
            pltpu.VMEM((2048, 128), F32),
            pltpu.VMEM((2048, 256), BF),
            pltpu.VMEM((256, 256), BF),
            pltpu.VMEM((256, 256), BF),
            pltpu.VMEM((128, 2048), BF),
            pltpu.VMEM((2048, 256), BF),
            pltpu.VMEM((128, 256), F32),
            pltpu.VMEM((2048, 128), BF),
            pltpu.VMEM((N, 8, 256), F32),
            pltpu.VMEM((N, 8, 256), F32),
            pltpu.VMEM((N, 16, 256), F32),
            pltpu.VMEM((N, 8, 128), F32),
            dma((N,)),
            dma((N,)),
            dma,
            dma((N,)),
            dma((N,)),
            dma((N,)),
            dma((N,)),
            dma((N,)),
            dma((N,)),
        ],
        compiler_params=pltpu.CompilerParams(
            collective_id=1, has_side_effects=True, vmem_limit_bytes=48 * 2**20
        ),
    )(tokens, ew_kv, ew_q, incoming, slots, norm_gains, embed_weight)
    return (
        noisy.reshape(1, 64, 128).transpose(0, 2, 1),
        att.reshape(1, 128, 2048),
        grads.reshape(128, 3, 1, 128),
        norms[0:2],
    )


def solution(mesh):
    return jax.shard_map(
        body,
        mesh=mesh,
        in_specs=(
            P("dp", "seq", None, None),
            P(),
            P(),
            P(),
            P(),
            P(),
            P("dp", "seq", None),
            P(),
            P(None, None, "seq", None),
            P(),
            P("dp", "seq", None),
        ),
        out_specs=(P("dp", "seq", None), P("dp", "seq", None), P("dp", None, "seq", None), P()),
        check_vma=False,
    )
```

```python
import jax
import jax.numpy as jnp
from jax import lax
from jax.experimental import pallas as pl
from jax.experimental.pallas import tpu as pltpu
from jax.sharding import PartitionSpec as P

F32 = jnp.float32
BF = jnp.bfloat16
N = 16
LN2 = 0.6931471805599453
MASKED = -300.0
EPS = 1e-06


def nn(a, b):
    return lax.dot_general(a, b, (((1,), (0,)), ((), ())), preferred_element_type=F32)


def nt(a, b):
    return lax.dot_general(a, b, (((1,), (1,)), ((), ())), preferred_element_type=F32)


def iota(shape, dim):
    return lax.broadcasted_iota(jnp.int32, shape, dim)


def block_of(i, size=128):
    return pl.ds(pl.multiple_of(i * size, size), size)


def peer(axis, k):
    return lax.rem(lax.axis_index(axis) + k + N, N)


def greet():
    barrier = pltpu.get_barrier_semaphore()

    def signal(**where):
        pl.semaphore_signal(barrier, inc=1, device_id=where, device_id_type=pl.DeviceIdType.MESH)

    def both(k, _):
        signal(dp=peer("dp", k))
        signal(seq=peer("seq", k))
        return 0

    lax.fori_loop(1, N, both, 0)
    for a in (-1, 1):
        for b in (-1, 1):
            signal(dp=peer("dp", a), seq=peer("seq", b))
    return lambda: pl.semaphore_wait(barrier, 2 * (N - 1) + 4)


def remote(src, dst, send, recv, **where):
    return pltpu.make_async_remote_copy(
        src_ref=src,
        dst_ref=dst,
        send_sem=send,
        recv_sem=recv,
        device_id=where,
        device_id_type=pl.DeviceIdType.MESH,
    )


def to_all(make):
    def start(k, _):
        make(k).start()
        return 0

    def wait(k, _):
        make(k).wait()
        return 0

    lax.fori_loop(1, N, start, 0)
    return lambda: lax.fori_loop(1, N, wait, 0)


def split(x):
    high = x.astype(BF)
    return high, (x - high.astype(F32)).astype(BF)


def whole(
    feat_h, wconv_h, frames_h, group_h, offset_h, times_h, noise_h, embed_h, proj_h, gains_h, cot,
    noisy, att, proj_out, norm_out,
    feat, wconv, ints, times_v, noise, embed, proj, gains,
    tab, actf, actp, conv, edge_out, late_out, own_late, edge_in, late_in, own_late_in, gath,
    tokens, incoming, ew, keys, vals, keys_t, vals_t, xq, xk, rq, rk, qx, gx, q_n, up_n, out_t, inv, even, odd, dss, dxq, dkv, outs,
    parts_kv, parts_q, landed_kv, sums, norms,
    in_sem, edge_send, edge_recv, dp_send, dp_recv, z_send, z_recv, sib_send, sib_recv,
    cot_send, cot_recv, own_sem, att_send, att_recv, kv_send, kv_recv, q_send, q_recv,
    nrm_send, nrm_recv, ag_send, ag_recv,
):
    slab = lax.axis_index("dp")
    row = lax.axis_index("seq")
    other = row + 1 - 2 * lax.rem(row, 2)
    fetches = []
    for src, dst in (
        (feat_h, feat), (wconv_h, wconv), (frames_h, ints.at[0]), (group_h, ints.at[1]), (offset_h, ints.at[2]),
        (times_h, times_v), (embed_h, embed), (proj_h, proj), (noise_h, noise), (gains_h, gains),
    ):
        fetches.append(pltpu.make_async_copy(src, dst, in_sem.at[len(fetches)]))
        fetches[-1].start()
    entered = greet()
    fetches[0].wait()
    for q in range(4):
        x = feat[:, q * 128 : q * 128 + 128].astype(F32)
        actf[q] = x / (1.0 + jnp.exp(-x))

    for part in range(4):
        r, b = part // 2, part % 2
        for t in range(8):
            for q in range(4):
                rows = actf[q, pl.ds(t * 64 + r * 32 + b, 16, stride=2), :]
                actp[pl.ds((part * 8 + t) * 16, 16), q * 128 : q * 128 + 128] = rows.astype(BF)
    fetches[1].wait()
    conv[...] = nt(wconv[...], actp[...])

    for i in range(2, 6):
        fetches[i].wait()
    tab[...] = jnp.zeros((8, 128), F32)
    for i in range(3):
        tab[i : i + 1, 0:32] = ints[i].astype(F32)
    tab[3:4, 0:32] = times_v[...]
    by_clip = tab[...].T
    frames, group, offset, times = [by_clip[0:32, i : i + 1] for i in range(4)]
    earlier = iota((32, 128), 1) < iota((32, 128), 0)
    starts = jnp.sum(jnp.where(earlier, tab[0:1, :], 0.0), axis=1, keepdims=True)
    lane = iota((1, 128), 1)
    slot_i = lax.shift_right_logical(lane, 4)
    col_i = lax.bitwise_and(lane, 15)
    slot = slot_i.astype(F32)
    in_slot = (group == slab.astype(F32)) & (slot >= offset) & (slot < offset + frames)
    over_clips = lambda v: jnp.sum(jnp.where(in_slot, v, 0.0), axis=0, keepdims=True)
    number = iota((32, 128), 0).astype(F32)
    usable = over_clips(1.0 + 0.0 * number)
    usable = jnp.where(usable > 0.0, 1.0, 0.0)
    segment = over_clips(number + 1.0) - 1.0
    source = over_clips(starts + slot - offset)
    level = over_clips(times + 0.0 * number)

    def own_start(frame):
        inside = (starts <= frame) & (frame < starts + frames)
        return jnp.sum(jnp.where(inside, starts, 0.0), axis=0, keepdims=True)

    here = slab.astype(F32) * 8.0 + slot
    after = here + 8.0
    start_here, start_after = own_start(here), own_start(after)
    keep = []
    for dt in range(3):
        main = (here - dt >= start_here) & (slot_i >= dt)
        late = (after - dt >= start_after) & (slot_i < dt)
        keep.append((jnp.where(main, 1.0, 0.0), jnp.where(late, 1.0, 0.0)))

    not_first = jnp.where(col_i > 0, 1.0, 0.0)
    not_last = jnp.where(col_i < 15, 1.0, 0.0)

    def tap(dt, dr, dw, r, ob):
        at = (((2 - dt) * 3 + dr + 1) * 3 + dw + 1) * 16
        b = (ob + dw) % 2
        piece = conv[at : at + 16, (r * 2 + b) * 128 : (r * 2 + b) * 128 + 128]
        if ob + dw == -1:
            return pltpu.roll(piece, 1, 1) * not_first
        if ob + dw == 2:
            return pltpu.roll(piece, 127, 1) * not_last
        return piece

    def sums_of(out_row, ob):
        main = late = None
        for dt in range(3):
            total = None
            for r in range(2):
                dr = r - out_row
                if abs(dr) <= 1:
                    for dw in range(-1, 2):
                        term = tap(dt, dr, dw, r, ob)
                        total = term if total is None else total + term
            if dt:
                total = pltpu.roll(total, 16 * dt, 1)
            m = total * keep[dt][0]
            main = m if main is None else main + m
            if dt:
                m = total * keep[dt][1]
                late = m if late is None else late + m
        return main, late

    for side, out_row in ((0, -1), (1, 2)):
        for ob in range(2):
            at = slice(ob * 16, ob * 16 + 16)
            edge_out[side, at, :], late_out[side, at, :] = sums_of(out_row, ob)
    mains = {}
    for a in range(2):
        for ob in range(2):
            at = slice((a * 2 + ob) * 16, (a * 2 + ob) * 16 + 16)
            mains[a, ob], own_late[at, :] = sums_of(a, ob)
    entered()

    routes = []
    for side, step in ((0, -1), (1, 1)):
        goes = (row > 0) if side == 0 else (row < N - 1)
        comes = (row < N - 1) if side == 0 else (row > 0)
        routes.append((
            remote(edge_out.at[side], edge_in.at[1 - side], edge_send.at[side], edge_recv.at[side], seq=peer("seq", step)),
            goes, comes, edge_in, 1 - side,
        ))
        routes.append((
            remote(
                late_out.at[side], late_in.at[1 - side], edge_send.at[2 + side], edge_recv.at[2 + side],
                dp=peer("dp", 1), seq=peer("seq", step),
            ),
            goes & (slab < N - 1), comes & (slab > 0), late_in, 1 - side,
        ))
    routes.append((
        remote(own_late, own_late_in.at[0], edge_send.at[4], edge_recv.at[4], dp=peer("dp", 1)),
        slab < N - 1, slab > 0, own_late_in, 0,
    ))
    for copy, goes, _, _, _ in routes:
        pl.when(goes)(copy.start)
    def cot_copy(k):
        return remote(
            cot.at[:, block_of(peer("seq", k))], incoming.at[block_of(row)], cot_send.at[k], cot_recv.at[k],
            seq=peer("seq", k),
        )

    own_cot = pltpu.make_async_copy(cot.at[:, block_of(row)], incoming.at[block_of(row)], own_sem.at[0])
    own_cot.start()
    for _, _, comes, dst, i in routes:

        @pl.when(jnp.logical_not(comes))
        def _():
            dst[i] = jnp.zeros(dst.shape[1:], F32)

    fetches[6].wait()
    fetches[7].wait()
    for j in range(3):
        high, low = split(nn(embed[...], proj[j]))
        ew[0:64, j * 128 : j * 128 + 128] = high
        ew[64:128, j * 128 : j * 128 + 128] = low
    base = source * 16.0 + col_i.astype(F32)
    select = jnp.where(iota((2048, 128), 0).astype(F32) == base, 1.0, 0.0).astype(BF)
    fetches[8].wait()
    fetches[9].wait()

    for copy, goes, comes, _, _ in routes:
        pl.when(goes)(copy.wait_send)
        pl.when(comes)(copy.wait_recv)
    for a in range(2):
        for ob in range(2):
            at = slice((a * 2 + ob) * 16, (a * 2 + ob) * 16 + 16)
            side = slice(ob * 16, ob * 16 + 16)
            total = mains[a, ob] + edge_in[a, side, :] + late_in[a, side, :] + own_late_in[0, at, :]
            gath[at, block_of(slab)] = total.astype(BF)
    mine = gath.at[:, block_of(slab)]
    gath_wait = to_all(lambda k: remote(mine, mine, dp_send.at[k], dp_recv.at[k], dp=peer("dp", k)))

    for k in (1, 15, 2, 14, 3, 13):
        cot_copy(k).start()
    gath_wait()

    made = usable * ((1.0 - level) * nn(gath[...], select) + level * noise[...].astype(F32))
    noisy[...] = made
    tokens[:, block_of(row)] = made.astype(BF)

    def tile_of(k):
        return tokens.at[:, block_of(peer("seq", -2 * k))]

    def to_chip(k):
        return remote(tile_of(0), tile_of(0), z_send.at[k], z_recv.at[k], seq=peer("seq", 2 * k))

    def to_other(k):
        return remote(tile_of(k), tile_of(k), sib_send.at[k], sib_recv.at[k], seq=other)

    for k in (4, 3, 5, 2, 6, 1, 7):
        to_chip(k).start()
    to_other(0).start()
    for k in (4, 12, 5, 11, 6, 10, 7, 9, 8):
        cot_copy(k).start()

    scale = 128.0**-0.5
    gain_q, gain_k = gains[0:1, :], gains[1:2, :]
    by_lane = jnp.broadcast_to(segment, (128, 128))
    by_row = by_lane.T
    key_mask = jnp.where(iota((128, 128), 1).astype(F32) - 1.0 == by_row, 0.0, MASKED).astype(BF)
    query_mask = jnp.where(iota((128, 128), 0).astype(F32) - 1.0 == by_lane, 1.0, 0.0).astype(BF)
    ones_two = jnp.where(iota((256, 128), 1) < 2, 1.0, 0.0).astype(BF)
    use_q = jnp.concatenate([usable, usable], axis=1)
    for p in range(N):
        qx[128:256, p * 128 : p * 128 + 128] = query_mask
        keys[p * 128 : p * 128 + 128, 128:256] = key_mask
    vals_t[128:144, :] = jnp.ones((16, 2048), BF)
    gx[128:256, :] = jnp.zeros((128, 2048), BF)

    chip = lax.div(row, 2)

    def place(i):
        return block_of(lax.rem(i, 2) * 4 + lax.div(i, 2), 256)

    def prepare(chip, i):
        at, qat = block_of(chip, 256), place(i)
        piece = tokens[:, at].astype(F32)
        tile = jnp.concatenate([piece, piece], axis=0).T.astype(BF)
        qkv = nn(tile, ew[...])
        x = qkv[:, 0:128]
        xq[qat, :] = x
        r = lax.rsqrt(jnp.mean(x * x, axis=1, keepdims=True) + EPS)
        rq[qat, :] = jnp.broadcast_to(r, (256, 128))
        query = x * (r * (scale / LN2)) * gain_q
        q_n[qat, :] = query.astype(BF)
        qx[0:128, qat] = query.T.astype(BF)
        x = qkv[:, 128:256]
        xk[at, :] = x
        r = lax.rsqrt(jnp.mean(x * x, axis=1, keepdims=True) + EPS)
        rk[at, :] = jnp.broadcast_to(r, (256, 128))
        key = x * r * gain_k
        keys[at, 0:128] = key.astype(BF)
        keys_t[:, at] = key.T.astype(BF)
        val = qkv[:, 256:384]
        vals[at, 0:128] = val.astype(BF)
        vals[at, 128:256] = ones_two
        vals_t[0:128, at] = val.T.astype(BF)

    def near(i):
        half = lax.div(i, 2)
        return jnp.where(lax.rem(i, 2) == 1, half + 1, 8 - half)

    def pass_on(i):
        to_chip(near(i)).wait_recv()
        to_other(near(i)).start()

    to_other(0).wait_recv()
    prepare(chip, 0)
    pass_on(1)

    def arrive(i, _):
        pass_on(i + 1)
        to_other(near(i)).wait_recv()
        prepare(lax.rem(chip + 8 - near(i), 8), lax.rem(8 - near(i), 8))
        return 0

    lax.fori_loop(1, 7, arrive, 0)
    to_other(4).wait_recv()
    prepare(lax.rem(chip + 4, 8), 4)

    def sent(k, _):
        to_chip(k).wait_send()
        to_other(k).wait_send()
        return 0

    lax.fori_loop(1, 8, sent, 0)
    to_other(0).wait_send()

    def send_out(p):
        return remote(outs.at[block_of(p)], att.at[:, block_of(row)], att_send.at[p], att_recv.at[row], seq=p)

    own_out = pltpu.make_async_copy(outs.at[block_of(row)], att.at[:, block_of(row)], own_sem.at[1])

    def score(i, buffer, c):
        kc = pl.ds(c * 512, 512)
        buffer[kc, block_of(lax.div(i, 2), 256)] = jnp.exp2(nn(keys[kc, :], qx[:, place(i)])).astype(BF)

    def output(i, buffer, c):
        kc = pl.ds(c * 512, 512)
        return nn(vals_t[:, kc], buffer[kc, block_of(lax.div(i, 2), 256)])

    def finish(i, out):
        at = place(i)
        inverse = 1.0 / out[128:129, :]
        out = out[0:128, :] * inverse
        inv[0:1, at] = inverse
        out_t[:, at] = out
        qb = lax.rem(chip + i, 8)
        outs[block_of(qb, 256), :] = (out * use_q).T.astype(BF)
        for p in (qb * 2, qb * 2 + 1):

            @pl.when(p != row)
            def _():
                send_out(p).start()

            @pl.when(p == row)
            def _():
                own_out.start()

    def pair(i, buffer, following):
        out = jnp.zeros((144, 256), F32)
        for c in range(4):
            score(i + 1, following, c)
            out = out + output(i, buffer, c)
        finish(i, out)

    for c in range(4):
        score(0, even, c)

    def forward(j, _):
        pair(2 * j, even, odd)
        pair(2 * j + 1, odd, even)
        return 0

    lax.fori_loop(0, 3, forward, 0)
    pair(6, even, odd)
    finish(7, nn(vals_t[...], odd[:, 768:1024]))

    def cot_wait(k, _):
        cot_copy(k).wait()
        return 0

    lax.fori_loop(1, N, cot_wait, 0)
    own_cot.wait()

    def incoming_rows(i, _):
        at = place(i)
        up = jnp.where(use_q > 0.0, incoming[block_of(lax.rem(chip + i, 8), 256), :].astype(F32).T, 0.0)
        up = (up * inv[0:1, at]).astype(BF)
        wide = up.astype(F32)
        delta = jnp.sum(wide * out_t[:, at], axis=0, keepdims=True)
        high, low = split(-delta)
        line = iota((16, 256), 0)
        extra = jnp.where(line == 0, high.astype(F32), jnp.where(line == 1, low.astype(F32), 0.0))
        gx[0:128, at] = up
        gx[128:144, at] = extra.astype(BF)
        up_n[at, :] = wide.T.astype(BF)
        return 0

    lax.fori_loop(0, 8, incoming_rows, 0)

    def rms_back(x, r, gain, grad):
        scaled = gain * grad
        mean = jnp.mean(x * scaled, axis=1, keepdims=True)
        return (r * (scaled - x * (r * r * mean))).astype(BF)

    def key_block(i, total):
        at = block_of(i, 256)
        for c in range(4):
            qc = pl.ds(c * 512, 512)
            e = (even, odd)[c // 2][at, c % 2 * 512 : c % 2 * 512 + 512]
            dss[at, qc] = (e.astype(F32) * nn(vals[at, :], gx[:, qc])).astype(BF)
        dkv[at, 128:256] = (nn(even[at, :], up_n[0:1024, :]) + nn(odd[at, :], up_n[1024:2048, :])).astype(BF)
        grad = nn(dss[at, :], q_n[...]) * LN2
        x, r = xk[at, :], rk[at, :]
        dkv[at, 0:128] = rms_back(x, r, gain_k, grad)
        return total + jnp.sum(grad * x * r, axis=0, keepdims=True)

    norm_k = lax.fori_loop(0, 8, key_block, jnp.zeros((1, 128), F32))
    part = nn(tokens[...], dkv[...])
    for j in range(N):
        parts_kv[j] = part[j // 2 * 8 : j // 2 * 8 + 8, j % 2 * 128 : j % 2 * 128 + 128]
    landed_kv[slab] = parts_kv[slab]
    kv_wait = to_all(
        lambda k: remote(
            parts_kv.at[peer("dp", k)], landed_kv.at[slab], kv_send.at[k], kv_recv.at[k], dp=peer("dp", k)
        )
    )

    line = iota((8, 128), 0)
    norms[row] = jnp.where(line == 0, norm_k * gain_k / gain_q, jnp.where(line == 1, norm_k, 0.0))
    norm_wait = to_all(
        lambda k: remote(norms.at[row], norms.at[row], nrm_send.at[k], nrm_recv.at[k], seq=peer("seq", k))
    )

    def query_back(i, _):
        at = place(i)
        grad = nn(keys_t[...], dss[:, at]).T * scale
        dxq[block_of(lax.rem(chip + i, 8), 256), :] = rms_back(xq[at, :], rq[at, :], gain_q, grad)
        return 0

    lax.fori_loop(0, 8, query_back, 0)
    parts_q[slab] = nn(tokens[...], dxq[...]).astype(BF)
    q_wait = to_all(
        lambda k: remote(parts_q.at[slab], parts_q.at[slab], q_send.at[k], q_recv.at[k], dp=peer("dp", k))
    )
    columns = embed[:, block_of(slab)].astype(F32).T.astype(BF)
    kv_wait()
    norm_wait()
    for i, buffer in enumerate((landed_kv, norms)):
        total = buffer[0]
        for j in range(1, N):
            total = total + buffer[j]
        sums[slab, i * 8 : i * 8 + 8, :] = total
    ag_wait = to_all(
        lambda k: remote(sums.at[slab], sums.at[slab], ag_send.at[k], ag_recv.at[k], dp=peer("dp", k))
    )

    def out_wait(p, _):
        @pl.when(p != row)
        def _():
            send_out(p).wait_send()
            remote(outs.at[block_of(p)], att.at[:, block_of(p)], att_send.at[p], att_recv.at[p], seq=p).wait_recv()

        return 0

    lax.fori_loop(0, N, out_wait, 0)
    own_out.wait()
    q_wait()
    whole_q = parts_q[0].astype(F32)
    for j in range(1, N):
        whole_q = whole_q + parts_q[j].astype(F32)
    ag_wait()
    whole_k = jnp.concatenate([sums[2 * b, 0:8, :] for b in range(8)], axis=0)
    whole_v = jnp.concatenate([sums[2 * b + 1, 0:8, :] for b in range(8)], axis=0)
    norm = sums[0, 8:16, :]
    for j in range(1, N):
        norm = norm + sums[j, 8:16, :]
    norm_out[...] = norm[0:2, :]
    for j, part in enumerate((whole_q, whole_k, whole_v)):
        high, low = split(part)
        proj_out[pl.ds(j, 128, stride=3), :] = nn(columns, high) + nn(columns, low)


def body(
    features,
    conv_weight,
    clip_frames,
    clip_group,
    clip_offset,
    clip_times,
    noise_tokens,
    embed_weight,
    attention_proj,
    norm_gains,
    cotangent,
):
    dma = pltpu.SemaphoreType.DMA
    vm = pltpu.VMEM
    in_hbm = lambda x: pltpu.with_memory_space_constraint(x, pltpu.HBM)
    noisy, att, grads, norms = pl.pallas_call(
        whole,
        name="whole",
        out_shape=(vm((64, 128), F32), vm((128, 2048), BF), vm((384, 128), F32), vm((2, 128), F32)),
        in_specs=[pl.BlockSpec(memory_space=pltpu.HBM)] * 11,
        out_specs=[pl.BlockSpec(memory_space=vm)] * 4,
        scratch_shapes=[
            vm((512, 512), BF), vm((432, 512), BF), vm((3, 1, 32), jnp.int32), vm((1, 32), F32), vm((64, 128), BF),
            vm((64, 2048), BF), vm((3, 2048, 128), BF), vm((2, 128), F32),
            vm((8, 128), F32), vm((4, 512, 128), F32), vm((512, 512), BF), vm((432, 512), F32),
            vm((2, 32, 128), F32), vm((2, 32, 128), F32), vm((64, 128), F32),
            vm((2, 32, 128), F32), vm((2, 32, 128), F32), vm((1, 64, 128), F32), vm((64, 2048), BF),
            vm((64, 2048), BF), vm((2048, 128), BF), vm((128, 384), BF),
            vm((2048, 256), BF), vm((2048, 256), BF), vm((128, 2048), BF), vm((144, 2048), BF),
            vm((2048, 128), F32), vm((2048, 128), F32), vm((2048, 128), F32), vm((2048, 128), F32), vm((256, 2048), BF), vm((256, 2048), BF),
            vm((2048, 128), BF), vm((2048, 128), BF), vm((128, 2048), F32), vm((8, 2048), F32),
            vm((2048, 1024), BF), vm((2048, 1024), BF), vm((2048, 2048), BF), vm((2048, 128), BF), vm((2048, 256), BF), vm((2048, 128), BF),
            vm((N, 8, 128), F32), vm((N, 64, 128), BF), vm((N, 8, 128), F32), vm((N, 16, 128), F32), vm((N, 8, 128), F32),
            dma((10,)), dma((5,)), dma((5,)), dma((N,)), dma((N,)), dma((8,)), dma((8,)), dma((8,)), dma((8,)),
            dma((N,)), dma((N,)), dma((2,)), dma((N,)), dma((N,)), dma((N,)), dma((N,)), dma((N,)), dma((N,)),
            dma((N,)), dma((N,)), dma((N,)), dma((N,)),
        ],
        compiler_params=pltpu.CompilerParams(collective_id=0, has_side_effects=True, vmem_limit_bytes=48 * 2**20),
    )(
        in_hbm(features.reshape(512, 512)),
        in_hbm(conv_weight.reshape(432, 512)),
        in_hbm(clip_frames.reshape(1, 32)),
        in_hbm(clip_group.reshape(1, 32)),
        in_hbm(clip_offset.reshape(1, 32)),
        in_hbm(clip_times.reshape(1, 32)),
        in_hbm(noise_tokens.transpose(0, 2, 1).reshape(64, 128)),
        in_hbm(embed_weight),
        in_hbm(attention_proj.transpose(1, 2, 0, 3).reshape(3, 2048, 128)),
        in_hbm(norm_gains),
        in_hbm(cotangent.reshape(128, 2048)),
    )
    return (
        noisy.reshape(1, 64, 128).transpose(0, 2, 1),
        att.reshape(1, 128, 2048),
        grads.reshape(128, 3, 1, 128),
        norms,
    )


def solution(mesh):
    return jax.shard_map(
        body,
        mesh=mesh,
        in_specs=(
            P("dp", "seq", None, None),
            P(),
            P(),
            P(),
            P(),
            P(),
            P("dp", "seq", None),
            P(),
            P(None, None, "seq", None),
            P(),
            P("dp", "seq", None),
        ),
        out_specs=(P("dp", "seq", None), P("dp", "seq", None), P("dp", None, "seq", None), P()),
        check_vma=False,
    )
```

```python
import jax
import jax.numpy as jnp
from jax import lax
from jax.experimental import pallas as pl
from jax.experimental.pallas import tpu as pltpu
from jax.sharding import PartitionSpec as P

F32 = jnp.float32
BF = jnp.bfloat16
N = 16
LN2 = 0.6931471805599453
MASKED = -300.0
EPS = 1e-06


def nn(a, b):
    return lax.dot_general(a, b, (((1,), (0,)), ((), ())), preferred_element_type=F32)


def nt(a, b):
    return lax.dot_general(a, b, (((1,), (1,)), ((), ())), preferred_element_type=F32)


def iota(shape, dim):
    return lax.broadcasted_iota(jnp.int32, shape, dim)


def block_of(i, size=128):
    return pl.ds(pl.multiple_of(i * size, size), size)


def peer(axis, k):
    return lax.rem(lax.axis_index(axis) + k + N, N)


def greet():
    barrier = pltpu.get_barrier_semaphore()

    def signal(**where):
        pl.semaphore_signal(barrier, inc=1, device_id=where, device_id_type=pl.DeviceIdType.MESH)

    def both(k, _):
        signal(dp=peer("dp", k))
        signal(seq=peer("seq", k))
        return 0

    lax.fori_loop(1, N, both, 0)
    for a in (-1, 1):
        for b in (-1, 1):
            signal(dp=peer("dp", a), seq=peer("seq", b))
    return lambda: pl.semaphore_wait(barrier, 2 * (N - 1) + 4)


def remote(src, dst, send, recv, **where):
    return pltpu.make_async_remote_copy(
        src_ref=src,
        dst_ref=dst,
        send_sem=send,
        recv_sem=recv,
        device_id=where,
        device_id_type=pl.DeviceIdType.MESH,
    )


def to_all(make):
    def start(k, _):
        make(k).start()
        return 0

    def wait(k, _):
        make(k).wait()
        return 0

    lax.fori_loop(1, N, start, 0)
    return lambda: lax.fori_loop(1, N, wait, 0)


def split(x):
    high = x.astype(BF)
    return high, (x - high.astype(F32)).astype(BF)


def whole(
    feat_h, wconv_h, frames_h, group_h, offset_h, times_h, noise_h, embed_h, proj_h, gains_h, cot,
    noisy, att, proj_out, norm_out,
    feat, wconv, ints, times_v, noise, embed, proj, gains,
    tab, actf, actp, conv, edge_out, late_out, own_late, edge_in, late_in, own_late_in, gath,
    tokens, incoming, ew, keys, vals, keys_t, vals_t, xq, xk, rq, rk, qx, gx, q_n, up_n, out_t, inv, even, odd, dss, dxq, dks, dvs, outs,
    parts, sums, norms,
    in_sem, edge_send, edge_recv, dp_send, dp_recv, z_send, z_recv, sib_send, sib_recv,
    cot_send, cot_recv, own_sem, att_send, att_recv, q_send, q_recv, k_send, k_recv, v_send, v_recv,
    nrm_send, nrm_recv, ag_send, ag_recv,
):
    slab = lax.axis_index("dp")
    row = lax.axis_index("seq")
    other = row + 1 - 2 * lax.rem(row, 2)
    fetches = []
    for src, dst in (
        (feat_h, feat), (wconv_h, wconv), (frames_h, ints.at[0]), (group_h, ints.at[1]), (offset_h, ints.at[2]),
        (times_h, times_v), (embed_h, embed), (proj_h, proj), (noise_h, noise), (gains_h, gains),
    ):
        fetches.append(pltpu.make_async_copy(src, dst, in_sem.at[len(fetches)]))
        fetches[-1].start()
    entered = greet()
    fetches[0].wait()
    for q in range(4):
        x = feat[:, q * 128 : q * 128 + 128].astype(F32)
        actf[q] = x / (1.0 + jnp.exp(-x))

    for part in range(4):
        r, b = part // 2, part % 2
        for t in range(8):
            for q in range(4):
                rows = actf[q, pl.ds(t * 64 + r * 32 + b, 16, stride=2), :]
                actp[pl.ds((part * 8 + t) * 16, 16), q * 128 : q * 128 + 128] = rows.astype(BF)
    fetches[1].wait()
    conv[...] = nt(wconv[...], actp[...])

    for i in range(2, 6):
        fetches[i].wait()
    tab[...] = jnp.zeros((8, 128), F32)
    for i in range(3):
        tab[i : i + 1, 0:32] = ints[i].astype(F32)
    tab[3:4, 0:32] = times_v[...]
    by_clip = tab[...].T
    frames, group, offset, times = [by_clip[0:32, i : i + 1] for i in range(4)]
    earlier = iota((32, 128), 1) < iota((32, 128), 0)
    starts = jnp.sum(jnp.where(earlier, tab[0:1, :], 0.0), axis=1, keepdims=True)
    lane = iota((1, 128), 1)
    slot_i = lax.shift_right_logical(lane, 4)
    col_i = lax.bitwise_and(lane, 15)
    slot = slot_i.astype(F32)
    in_slot = (group == slab.astype(F32)) & (slot >= offset) & (slot < offset + frames)
    over_clips = lambda v: jnp.sum(jnp.where(in_slot, v, 0.0), axis=0, keepdims=True)
    number = iota((32, 128), 0).astype(F32)
    usable = over_clips(1.0 + 0.0 * number)
    usable = jnp.where(usable > 0.0, 1.0, 0.0)
    segment = over_clips(number + 1.0) - 1.0
    source = over_clips(starts + slot - offset)
    level = over_clips(times + 0.0 * number)

    def own_start(frame):
        inside = (starts <= frame) & (frame < starts + frames)
        return jnp.sum(jnp.where(inside, starts, 0.0), axis=0, keepdims=True)

    here = slab.astype(F32) * 8.0 + slot
    after = here + 8.0
    start_here, start_after = own_start(here), own_start(after)
    keep = []
    for dt in range(3):
        main = (here - dt >= start_here) & (slot_i >= dt)
        late = (after - dt >= start_after) & (slot_i < dt)
        keep.append((jnp.where(main, 1.0, 0.0), jnp.where(late, 1.0, 0.0)))

    not_first = jnp.where(col_i > 0, 1.0, 0.0)
    not_last = jnp.where(col_i < 15, 1.0, 0.0)

    def tap(dt, dr, dw, r, ob):
        at = (((2 - dt) * 3 + dr + 1) * 3 + dw + 1) * 16
        b = (ob + dw) % 2
        piece = conv[at : at + 16, (r * 2 + b) * 128 : (r * 2 + b) * 128 + 128]
        if ob + dw == -1:
            return pltpu.roll(piece, 1, 1) * not_first
        if ob + dw == 2:
            return pltpu.roll(piece, 127, 1) * not_last
        return piece

    def sums_of(out_row, ob):
        main = late = None
        for dt in range(3):
            total = None
            for r in range(2):
                dr = r - out_row
                if abs(dr) <= 1:
                    for dw in range(-1, 2):
                        term = tap(dt, dr, dw, r, ob)
                        total = term if total is None else total + term
            if dt:
                total = pltpu.roll(total, 16 * dt, 1)
            m = total * keep[dt][0]
            main = m if main is None else main + m
            if dt:
                m = total * keep[dt][1]
                late = m if late is None else late + m
        return main, late

    for side, out_row in ((0, -1), (1, 2)):
        for ob in range(2):
            at = slice(ob * 16, ob * 16 + 16)
            edge_out[side, at, :], late_out[side, at, :] = sums_of(out_row, ob)
    mains = {}
    for a in range(2):
        for ob in range(2):
            at = slice((a * 2 + ob) * 16, (a * 2 + ob) * 16 + 16)
            mains[a, ob], own_late[at, :] = sums_of(a, ob)
    entered()

    routes = []
    for side, step in ((0, -1), (1, 1)):
        goes = (row > 0) if side == 0 else (row < N - 1)
        comes = (row < N - 1) if side == 0 else (row > 0)
        routes.append((
            remote(edge_out.at[side], edge_in.at[1 - side], edge_send.at[side], edge_recv.at[side], seq=peer("seq", step)),
            goes, comes, edge_in, 1 - side,
        ))
        routes.append((
            remote(
                late_out.at[side], late_in.at[1 - side], edge_send.at[2 + side], edge_recv.at[2 + side],
                dp=peer("dp", 1), seq=peer("seq", step),
            ),
            goes & (slab < N - 1), comes & (slab > 0), late_in, 1 - side,
        ))
    routes.append((
        remote(own_late, own_late_in.at[0], edge_send.at[4], edge_recv.at[4], dp=peer("dp", 1)),
        slab < N - 1, slab > 0, own_late_in, 0,
    ))
    for copy, goes, _, _, _ in routes:
        pl.when(goes)(copy.start)
    def cot_copy(k):
        return remote(
            cot.at[:, block_of(peer("seq", k))], incoming.at[block_of(row)], cot_send.at[k], cot_recv.at[k],
            seq=peer("seq", k),
        )

    own_cot = pltpu.make_async_copy(cot.at[:, block_of(row)], incoming.at[block_of(row)], own_sem.at[0])
    own_cot.start()
    for _, _, comes, dst, i in routes:

        @pl.when(jnp.logical_not(comes))
        def _():
            dst[i] = jnp.zeros(dst.shape[1:], F32)

    fetches[6].wait()
    fetches[7].wait()
    for j in range(3):
        high, low = split(nn(embed[...], proj[j]))
        ew[0:64, j * 128 : j * 128 + 128] = high
        ew[64:128, j * 128 : j * 128 + 128] = low
    base = source * 16.0 + col_i.astype(F32)
    select = jnp.where(iota((2048, 128), 0).astype(F32) == base, 1.0, 0.0).astype(BF)
    fetches[8].wait()
    fetches[9].wait()

    for copy, goes, comes, _, _ in routes:
        pl.when(goes)(copy.wait_send)
        pl.when(comes)(copy.wait_recv)
    for a in range(2):
        for ob in range(2):
            at = slice((a * 2 + ob) * 16, (a * 2 + ob) * 16 + 16)
            side = slice(ob * 16, ob * 16 + 16)
            total = mains[a, ob] + edge_in[a, side, :] + late_in[a, side, :] + own_late_in[0, at, :]
            gath[at, block_of(slab)] = total.astype(BF)
    mine = gath.at[:, block_of(slab)]
    gath_wait = to_all(lambda k: remote(mine, mine, dp_send.at[k], dp_recv.at[k], dp=peer("dp", k)))

    for k in (1, 15, 2, 14, 3, 13):
        cot_copy(k).start()
    gath_wait()

    made = usable * ((1.0 - level) * nn(gath[...], select) + level * noise[...].astype(F32))
    noisy[...] = made
    tokens[:, block_of(row)] = made.astype(BF)

    def tile_of(k):
        return tokens.at[:, block_of(peer("seq", -2 * k))]

    def to_chip(k):
        return remote(tile_of(0), tile_of(0), z_send.at[k], z_recv.at[k], seq=peer("seq", 2 * k))

    def to_other(k):
        return remote(tile_of(k), tile_of(k), sib_send.at[k], sib_recv.at[k], seq=other)

    for k in (4, 3, 5, 2, 6, 1, 7):
        to_chip(k).start()
    to_other(0).start()
    for k in (4, 12, 5, 11, 6, 10, 7, 9, 8):
        cot_copy(k).start()

    scale = 128.0**-0.5
    gain_q, gain_k = gains[0:1, :], gains[1:2, :]
    by_lane = jnp.broadcast_to(segment, (128, 128))
    by_row = by_lane.T
    key_mask = jnp.where(iota((128, 128), 1).astype(F32) - 1.0 == by_row, 0.0, MASKED).astype(BF)
    query_mask = jnp.where(iota((128, 128), 0).astype(F32) - 1.0 == by_lane, 1.0, 0.0).astype(BF)
    ones_two = jnp.where(iota((256, 128), 1) < 2, 1.0, 0.0).astype(BF)
    use_q = jnp.concatenate([usable, usable], axis=1)
    for p in range(N):
        qx[128:256, p * 128 : p * 128 + 128] = query_mask
        keys[p * 128 : p * 128 + 128, 128:256] = key_mask
    vals_t[128:144, :] = jnp.ones((16, 2048), BF)
    gx[128:256, :] = jnp.zeros((128, 2048), BF)

    chip = lax.div(row, 2)

    def place(i):
        return block_of(lax.rem(i, 2) * 4 + lax.div(i, 2), 256)

    def prepare(chip, i):
        at, qat = block_of(chip, 256), place(i)
        piece = tokens[:, at].astype(F32)
        tile = jnp.concatenate([piece, piece], axis=0).T.astype(BF)
        qkv = nn(tile, ew[...])
        x = qkv[:, 0:128]
        xq[qat, :] = x
        r = lax.rsqrt(jnp.mean(x * x, axis=1, keepdims=True) + EPS)
        rq[qat, :] = jnp.broadcast_to(r, (256, 128))
        query = x * (r * (scale / LN2)) * gain_q
        q_n[qat, :] = query.astype(BF)
        qx[0:128, qat] = query.T.astype(BF)
        x = qkv[:, 128:256]
        xk[at, :] = x
        r = lax.rsqrt(jnp.mean(x * x, axis=1, keepdims=True) + EPS)
        rk[at, :] = jnp.broadcast_to(r, (256, 128))
        key = x * r * gain_k
        keys[at, 0:128] = key.astype(BF)
        keys_t[:, at] = key.T.astype(BF)
        val = qkv[:, 256:384]
        vals[at, 0:128] = val.astype(BF)
        vals[at, 128:256] = ones_two
        vals_t[0:128, at] = val.T.astype(BF)

    def near(i):
        half = lax.div(i, 2)
        return jnp.where(lax.rem(i, 2) == 1, half + 1, 8 - half)

    def pass_on(i):
        to_chip(near(i)).wait_recv()
        to_other(near(i)).start()

    to_other(0).wait_recv()
    prepare(chip, 0)
    pass_on(1)

    def arrive(i, _):
        pass_on(i + 1)
        to_other(near(i)).wait_recv()
        prepare(lax.rem(chip + 8 - near(i), 8), lax.rem(8 - near(i), 8))
        return 0

    lax.fori_loop(1, 7, arrive, 0)
    to_other(4).wait_recv()
    prepare(lax.rem(chip + 4, 8), 4)

    def sent(k, _):
        to_chip(k).wait_send()
        to_other(k).wait_send()
        return 0

    lax.fori_loop(1, 8, sent, 0)
    to_other(0).wait_send()

    def send_out(p):
        return remote(outs.at[block_of(p)], att.at[:, block_of(row)], att_send.at[p], att_recv.at[row], seq=p)

    own_out = pltpu.make_async_copy(outs.at[block_of(row)], att.at[:, block_of(row)], own_sem.at[1])

    def score(i, buffer, c):
        kc = pl.ds(c * 512, 512)
        buffer[kc, block_of(lax.div(i, 2), 256)] = jnp.exp2(nn(keys[kc, :], qx[:, place(i)])).astype(BF)

    def output(i, buffer, c):
        kc = pl.ds(c * 512, 512)
        return nn(vals_t[:, kc], buffer[kc, block_of(lax.div(i, 2), 256)])

    def finish(i, out):
        at = place(i)
        inverse = 1.0 / out[128:129, :]
        out = out[0:128, :] * inverse
        inv[0:1, at] = inverse
        out_t[:, at] = out
        qb = lax.rem(chip + i, 8)
        outs[block_of(qb, 256), :] = (out * use_q).T.astype(BF)
        for p in (qb * 2, qb * 2 + 1):

            @pl.when(p != row)
            def _():
                send_out(p).start()

            @pl.when(p == row)
            def _():
                own_out.start()

    def pair(i, buffer, following):
        out = jnp.zeros((144, 256), F32)
        for c in range(4):
            score(i + 1, following, c)
            out = out + output(i, buffer, c)
        finish(i, out)

    for c in range(4):
        score(0, even, c)

    def forward(j, _):
        pair(2 * j, even, odd)
        pair(2 * j + 1, odd, even)
        return 0

    lax.fori_loop(0, 3, forward, 0)
    pair(6, even, odd)
    finish(7, nn(vals_t[...], odd[:, 768:1024]))

    def cot_wait(k, _):
        cot_copy(k).wait()
        return 0

    lax.fori_loop(1, N, cot_wait, 0)
    own_cot.wait()

    def incoming_rows(i, _):
        at = place(i)
        up = jnp.where(use_q > 0.0, incoming[block_of(lax.rem(chip + i, 8), 256), :].astype(F32).T, 0.0)
        up = (up * inv[0:1, at]).astype(BF)
        wide = up.astype(F32)
        delta = jnp.sum(wide * out_t[:, at], axis=0, keepdims=True)
        high, low = split(-delta)
        line = iota((16, 256), 0)
        extra = jnp.where(line == 0, high.astype(F32), jnp.where(line == 1, low.astype(F32), 0.0))
        gx[0:128, at] = up
        gx[128:144, at] = extra.astype(BF)
        up_n[at, :] = wide.T.astype(BF)
        return 0

    lax.fori_loop(0, 8, incoming_rows, 0)

    def rms_back(x, r, gain, grad):
        scaled = gain * grad
        mean = jnp.mean(x * scaled, axis=1, keepdims=True)
        return (r * (scaled - x * (r * r * mean))).astype(BF)

    def score_back(i, _):
        at = block_of(i, 512)
        for c in range(4):
            qc = pl.ds(c * 512, 512)
            e = (even, odd)[c // 2][at, c % 2 * 512 : c % 2 * 512 + 512]
            dss[at, qc] = (e.astype(F32) * nn(vals[at, :], gx[:, qc])).astype(BF)
        return 0

    def query_back(i, total):
        at = block_of(i, 1024)
        grad = nn(keys_t[...], dss[:, at]).T * scale
        x, r = xq[at, :], rq[at, :]
        back = rms_back(x, r, gain_q, grad)
        for n in range(1024 // 256):
            place_n = i * 4 + n
            block = lax.rem(place_n, 4) * 2 + lax.div(place_n, 4)
            dxq[block_of(lax.rem(chip + block, 8), 256), :] = back[n * 256 : n * 256 + 256, :]
        return total + jnp.sum(grad * x * r, axis=0, keepdims=True)

    def value_back(i, _):
        at = block_of(i, 1024)
        dvs[at, :] = (nn(even[at, :], up_n[0:1024, :]) + nn(odd[at, :], up_n[1024:2048, :])).astype(BF)
        return 0

    def key_back(i, _):
        at = block_of(i, 1024)
        dks[at, :] = rms_back(xk[at, :], rk[at, :], gain_k, nn(dss[at, :], q_n[...]) * LN2)
        return 0

    def share(j, grads, send, recv):
        parts[j, slab] = nn(tokens[...], grads[...]).astype(BF)
        mine = parts.at[j, slab]
        return to_all(lambda k: remote(mine, mine, send.at[k], recv.at[k], dp=peer("dp", k)))

    lax.fori_loop(0, 4, score_back, 0)
    norm_q = lax.fori_loop(0, 2, query_back, jnp.zeros((1, 128), F32))
    line = iota((8, 128), 0)
    norms[row] = jnp.where(line == 0, norm_q, jnp.where(line == 1, norm_q * gain_q / gain_k, 0.0))
    norm_wait = to_all(
        lambda k: remote(norms.at[row], norms.at[row], nrm_send.at[k], nrm_recv.at[k], seq=peer("seq", k))
    )
    q_wait = share(0, dxq, q_send, q_recv)
    lax.fori_loop(0, 2, value_back, 0)
    v_wait = share(2, dvs, v_send, v_recv)
    lax.fori_loop(0, 2, key_back, 0)
    k_wait = share(1, dks, k_send, k_recv)
    norm_wait()
    norm = norms[0]
    for j in range(1, N):
        norm = norm + norms[j]
    sums[slab] = norm
    ag_wait = to_all(
        lambda k: remote(sums.at[slab], sums.at[slab], ag_send.at[k], ag_recv.at[k], dp=peer("dp", k))
    )
    columns = embed[:, block_of(slab)].astype(F32).T.astype(BF)

    def project(j):
        whole_sum = parts[j, 0].astype(F32)
        for i in range(1, N):
            whole_sum = whole_sum + parts[j, i].astype(F32)
        high, low = split(whole_sum)
        proj_out[pl.ds(j, 128, stride=3), :] = nn(columns, high) + nn(columns, low)

    def out_wait(p, _):
        @pl.when(p != row)
        def _():
            send_out(p).wait_send()
            remote(outs.at[block_of(p)], att.at[:, block_of(p)], att_send.at[p], att_recv.at[p], seq=p).wait_recv()

        return 0

    lax.fori_loop(0, N, out_wait, 0)
    own_out.wait()
    q_wait()
    project(0)
    v_wait()
    project(2)
    k_wait()
    project(1)
    ag_wait()
    norm = sums[0]
    for j in range(1, N):
        norm = norm + sums[j]
    norm_out[...] = norm[0:2, :]


def body(
    features,
    conv_weight,
    clip_frames,
    clip_group,
    clip_offset,
    clip_times,
    noise_tokens,
    embed_weight,
    attention_proj,
    norm_gains,
    cotangent,
):
    dma = pltpu.SemaphoreType.DMA
    vm = pltpu.VMEM
    in_hbm = lambda x: pltpu.with_memory_space_constraint(x, pltpu.HBM)
    noisy, att, grads, norms = pl.pallas_call(
        whole,
        name="whole",
        out_shape=(vm((64, 128), F32), vm((128, 2048), BF), vm((384, 128), F32), vm((2, 128), F32)),
        in_specs=[pl.BlockSpec(memory_space=pltpu.HBM)] * 11,
        out_specs=[pl.BlockSpec(memory_space=vm)] * 4,
        scratch_shapes=[
            vm((512, 512), BF), vm((432, 512), BF), vm((3, 1, 32), jnp.int32), vm((1, 32), F32), vm((64, 128), BF),
            vm((64, 2048), BF), vm((3, 2048, 128), BF), vm((2, 128), F32),
            vm((8, 128), F32), vm((4, 512, 128), F32), vm((512, 512), BF), vm((432, 512), F32),
            vm((2, 32, 128), F32), vm((2, 32, 128), F32), vm((64, 128), F32),
            vm((2, 32, 128), F32), vm((2, 32, 128), F32), vm((1, 64, 128), F32), vm((64, 2048), BF),
            vm((64, 2048), BF), vm((2048, 128), BF), vm((128, 384), BF),
            vm((2048, 256), BF), vm((2048, 256), BF), vm((128, 2048), BF), vm((144, 2048), BF),
            vm((2048, 128), F32), vm((2048, 128), F32), vm((2048, 128), F32), vm((2048, 128), F32), vm((256, 2048), BF), vm((256, 2048), BF),
            vm((2048, 128), BF), vm((2048, 128), BF), vm((128, 2048), F32), vm((8, 2048), F32),
            vm((2048, 1024), BF), vm((2048, 1024), BF), vm((2048, 2048), BF), vm((2048, 128), BF), vm((2048, 128), BF), vm((2048, 128), BF), vm((2048, 128), BF),
            vm((3, N, 64, 128), BF), vm((N, 8, 128), F32), vm((N, 8, 128), F32),
            dma((10,)), dma((5,)), dma((5,)), dma((N,)), dma((N,)), dma((8,)), dma((8,)), dma((8,)), dma((8,)),
            dma((N,)), dma((N,)), dma((2,)), dma((N,)), dma((N,)), dma((N,)), dma((N,)), dma((N,)), dma((N,)),
            dma((N,)), dma((N,)), dma((N,)), dma((N,)), dma((N,)), dma((N,)),
        ],
        compiler_params=pltpu.CompilerParams(collective_id=0, has_side_effects=True, vmem_limit_bytes=48 * 2**20),
    )(
        in_hbm(features.reshape(512, 512)),
        in_hbm(conv_weight.reshape(432, 512)),
        in_hbm(clip_frames.reshape(1, 32)),
        in_hbm(clip_group.reshape(1, 32)),
        in_hbm(clip_offset.reshape(1, 32)),
        in_hbm(clip_times.reshape(1, 32)),
        in_hbm(noise_tokens.transpose(0, 2, 1).reshape(64, 128)),
        in_hbm(embed_weight),
        in_hbm(attention_proj.transpose(1, 2, 0, 3).reshape(3, 2048, 128)),
        in_hbm(norm_gains),
        in_hbm(cotangent.reshape(128, 2048)),
    )
    return (
        noisy.reshape(1, 64, 128).transpose(0, 2, 1),
        att.reshape(1, 128, 2048),
        grads.reshape(128, 3, 1, 128),
        norms,
    )


def solution(mesh):
    return jax.shard_map(
        body,
        mesh=mesh,
        in_specs=(
            P("dp", "seq", None, None),
            P(),
            P(),
            P(),
            P(),
            P(),
            P("dp", "seq", None),
            P(),
            P(None, None, "seq", None),
            P(),
            P("dp", "seq", None),
        ),
        out_specs=(P("dp", "seq", None), P("dp", "seq", None), P("dp", None, "seq", None), P()),
        check_vma=False,
    )
```

```python
import jax
import jax.numpy as jnp
from jax import lax
from jax.experimental import pallas as pl
from jax.experimental.pallas import tpu as pltpu
from jax.sharding import PartitionSpec as P

F32 = jnp.float32
BF = jnp.bfloat16
N = 16
LN2 = 0.6931471805599453
MASKED = -300.0
EPS = 1e-06


def nn(a, b):
    return lax.dot_general(a, b, (((1,), (0,)), ((), ())), preferred_element_type=F32)


def nt(a, b):
    return lax.dot_general(a, b, (((1,), (1,)), ((), ())), preferred_element_type=F32)


def iota(shape, dim):
    return lax.broadcasted_iota(jnp.int32, shape, dim)


def block_of(i, size=128):
    return pl.ds(pl.multiple_of(i * size, size), size)


def peer(axis, k):
    return lax.rem(lax.axis_index(axis) + k + N, N)


def greet():
    barrier = pltpu.get_barrier_semaphore()

    def signal(**where):
        pl.semaphore_signal(barrier, inc=1, device_id=where, device_id_type=pl.DeviceIdType.MESH)

    def both(k, _):
        signal(dp=peer("dp", k))
        signal(seq=peer("seq", k))
        return 0

    lax.fori_loop(1, N, both, 0)
    for a in (-1, 1):
        for b in (-1, 1):
            signal(dp=peer("dp", a), seq=peer("seq", b))
    return lambda: pl.semaphore_wait(barrier, 2 * (N - 1) + 4)


def remote(src, dst, send, recv, **where):
    return pltpu.make_async_remote_copy(
        src_ref=src,
        dst_ref=dst,
        send_sem=send,
        recv_sem=recv,
        device_id=where,
        device_id_type=pl.DeviceIdType.MESH,
    )


def to_all(make):
    def start(k, _):
        make(k).start()
        return 0

    def wait(k, _):
        make(k).wait()
        return 0

    lax.fori_loop(1, N, start, 0)
    return lambda: lax.fori_loop(1, N, wait, 0)


def split(x):
    high = x.astype(BF)
    return high, (x - high.astype(F32)).astype(BF)


def whole(
    feat_h, wconv_h, frames_h, group_h, offset_h, times_h, noise_h, embed_h, proj_h, gains_h, cot,
    noisy, att, proj_out, norm_out,
    feat, wconv, ints, times_v, noise, embed, proj, gains,
    tab, actf, actp, conv, edge_out, late_out, own_late, edge_in, late_in, own_late_in, gath,
    tokens, incoming, ew, keys, vals, keys_t, vals_t, xq, xk, rq, rk, qx, gx, q_n, up_n, out_t, inv, even, odd, dss, dxq, dks, dvs, outs,
    parts, sums, norms,
    in_sem, edge_send, edge_recv, dp_send, dp_recv, z_send, z_recv, sib_send, sib_recv,
    cot_send, cot_recv, own_sem, att_send, att_recv, q_send, q_recv, k_send, k_recv, v_send, v_recv,
    nrm_send, nrm_recv, ag_send, ag_recv,
):
    slab = lax.axis_index("dp")
    row = lax.axis_index("seq")
    other = row + 1 - 2 * lax.rem(row, 2)
    fetches = []
    for src, dst in (
        (feat_h, feat), (wconv_h, wconv), (frames_h, ints.at[0]), (group_h, ints.at[1]), (offset_h, ints.at[2]),
        (times_h, times_v), (embed_h, embed), (proj_h, proj), (noise_h, noise), (gains_h, gains),
    ):
        fetches.append(pltpu.make_async_copy(src, dst, in_sem.at[len(fetches)]))
        fetches[-1].start()
    entered = greet()
    fetches[0].wait()
    for q in range(4):
        x = feat[:, q * 128 : q * 128 + 128].astype(F32)
        actf[q] = x / (1.0 + jnp.exp(-x))

    for part in range(4):
        r, b = part // 2, part % 2
        for t in range(8):
            for q in range(4):
                rows = actf[q, pl.ds(t * 64 + r * 32 + b, 16, stride=2), :]
                actp[pl.ds((part * 8 + t) * 16, 16), q * 128 : q * 128 + 128] = rows.astype(BF)
    fetches[1].wait()
    conv[...] = nt(wconv[...], actp[...])

    for i in range(2, 6):
        fetches[i].wait()
    tab[...] = jnp.zeros((8, 128), F32)
    for i in range(3):
        tab[i : i + 1, 0:32] = ints[i].astype(F32)
    tab[3:4, 0:32] = times_v[...]
    by_clip = tab[...].T
    frames, group, offset, times = [by_clip[0:32, i : i + 1] for i in range(4)]
    earlier = iota((32, 128), 1) < iota((32, 128), 0)
    starts = jnp.sum(jnp.where(earlier, tab[0:1, :], 0.0), axis=1, keepdims=True)
    lane = iota((1, 128), 1)
    slot_i = lax.shift_right_logical(lane, 4)
    col_i = lax.bitwise_and(lane, 15)
    slot = slot_i.astype(F32)
    in_slot = (group == slab.astype(F32)) & (slot >= offset) & (slot < offset + frames)
    over_clips = lambda v: jnp.sum(jnp.where(in_slot, v, 0.0), axis=0, keepdims=True)
    number = iota((32, 128), 0).astype(F32)
    usable = over_clips(1.0 + 0.0 * number)
    usable = jnp.where(usable > 0.0, 1.0, 0.0)
    segment = over_clips(number + 1.0) - 1.0
    source = over_clips(starts + slot - offset)
    level = over_clips(times + 0.0 * number)

    def own_start(frame):
        inside = (starts <= frame) & (frame < starts + frames)
        return jnp.sum(jnp.where(inside, starts, 0.0), axis=0, keepdims=True)

    here = slab.astype(F32) * 8.0 + slot
    after = here + 8.0
    start_here, start_after = own_start(here), own_start(after)
    keep = []
    for dt in range(3):
        main = (here - dt >= start_here) & (slot_i >= dt)
        late = (after - dt >= start_after) & (slot_i < dt)
        keep.append((jnp.where(main, 1.0, 0.0), jnp.where(late, 1.0, 0.0)))

    not_first = jnp.where(col_i > 0, 1.0, 0.0)
    not_last = jnp.where(col_i < 15, 1.0, 0.0)

    def tap(dt, dr, dw, r, ob):
        at = (((2 - dt) * 3 + dr + 1) * 3 + dw + 1) * 16
        b = (ob + dw) % 2
        piece = conv[at : at + 16, (r * 2 + b) * 128 : (r * 2 + b) * 128 + 128]
        if ob + dw == -1:
            return pltpu.roll(piece, 1, 1) * not_first
        if ob + dw == 2:
            return pltpu.roll(piece, 127, 1) * not_last
        return piece

    def sums_of(out_row, ob):
        main = late = None
        for dt in range(3):
            total = None
            for r in range(2):
                dr = r - out_row
                if abs(dr) <= 1:
                    for dw in range(-1, 2):
                        term = tap(dt, dr, dw, r, ob)
                        total = term if total is None else total + term
            if dt:
                total = pltpu.roll(total, 16 * dt, 1)
            m = total * keep[dt][0]
            main = m if main is None else main + m
            if dt:
                m = total * keep[dt][1]
                late = m if late is None else late + m
        return main, late

    for side, out_row in ((0, -1), (1, 2)):
        for ob in range(2):
            at = slice(ob * 16, ob * 16 + 16)
            edge_out[side, at, :], late_out[side, at, :] = sums_of(out_row, ob)
    mains = {}
    for a in range(2):
        for ob in range(2):
            at = slice((a * 2 + ob) * 16, (a * 2 + ob) * 16 + 16)
            mains[a, ob], own_late[at, :] = sums_of(a, ob)
    entered()

    routes = []
    for side, step in ((0, -1), (1, 1)):
        goes = (row > 0) if side == 0 else (row < N - 1)
        comes = (row < N - 1) if side == 0 else (row > 0)
        routes.append((
            remote(edge_out.at[side], edge_in.at[1 - side], edge_send.at[side], edge_recv.at[side], seq=peer("seq", step)),
            goes, comes, edge_in, 1 - side,
        ))
        routes.append((
            remote(
                late_out.at[side], late_in.at[1 - side], edge_send.at[2 + side], edge_recv.at[2 + side],
                dp=peer("dp", 1), seq=peer("seq", step),
            ),
            goes & (slab < N - 1), comes & (slab > 0), late_in, 1 - side,
        ))
    routes.append((
        remote(own_late, own_late_in.at[0], edge_send.at[4], edge_recv.at[4], dp=peer("dp", 1)),
        slab < N - 1, slab > 0, own_late_in, 0,
    ))
    for copy, goes, _, _, _ in routes:
        pl.when(goes)(copy.start)
    def cot_copy(k):
        return remote(
            cot.at[:, block_of(peer("seq", k))], incoming.at[block_of(row)], cot_send.at[k], cot_recv.at[k],
            seq=peer("seq", k),
        )

    own_cot = pltpu.make_async_copy(cot.at[:, block_of(row)], incoming.at[block_of(row)], own_sem.at[0])
    own_cot.start()
    for _, _, comes, dst, i in routes:

        @pl.when(jnp.logical_not(comes))
        def _():
            dst[i] = jnp.zeros(dst.shape[1:], F32)

    fetches[6].wait()
    fetches[7].wait()
    for j in range(3):
        high, low = split(nn(embed[...], proj[j]))
        ew[0:64, j * 128 : j * 128 + 128] = high
        ew[64:128, j * 128 : j * 128 + 128] = low
    base = source * 16.0 + col_i.astype(F32)
    select = jnp.where(iota((2048, 128), 0).astype(F32) == base, 1.0, 0.0).astype(BF)
    fetches[8].wait()
    fetches[9].wait()

    for copy, goes, comes, _, _ in routes:
        pl.when(goes)(copy.wait_send)
        pl.when(comes)(copy.wait_recv)
    for a in range(2):
        for ob in range(2):
            at = slice((a * 2 + ob) * 16, (a * 2 + ob) * 16 + 16)
            side = slice(ob * 16, ob * 16 + 16)
            total = mains[a, ob] + edge_in[a, side, :] + late_in[a, side, :] + own_late_in[0, at, :]
            gath[at, block_of(slab)] = total.astype(BF)
    mine = gath.at[:, block_of(slab)]
    gath_wait = to_all(lambda k: remote(mine, mine, dp_send.at[k], dp_recv.at[k], dp=peer("dp", k)))

    for k in (1, 15, 2, 14, 3, 13):
        cot_copy(k).start()
    gath_wait()

    made = usable * ((1.0 - level) * nn(gath[...], select) + level * noise[...].astype(F32))
    noisy[...] = made
    tokens[:, block_of(row)] = made.astype(BF)

    def tile_of(k):
        return tokens.at[:, block_of(peer("seq", -2 * k))]

    def to_chip(k):
        return remote(tile_of(0), tile_of(0), z_send.at[k], z_recv.at[k], seq=peer("seq", 2 * k))

    def to_other(k):
        return remote(tile_of(k), tile_of(k), sib_send.at[k], sib_recv.at[k], seq=other)

    for k in (4, 3, 5, 2, 6, 1, 7):
        to_chip(k).start()
    to_other(0).start()
    for k in (4, 12, 5, 11, 6, 10, 7, 9, 8):
        cot_copy(k).start()

    scale = 128.0**-0.5
    gain_q, gain_k = gains[0:1, :], gains[1:2, :]
    by_lane = jnp.broadcast_to(segment, (128, 128))
    by_row = by_lane.T
    key_mask = jnp.where(iota((128, 128), 1).astype(F32) - 1.0 == by_row, 0.0, MASKED).astype(BF)
    query_mask = jnp.where(iota((128, 128), 0).astype(F32) - 1.0 == by_lane, 1.0, 0.0).astype(BF)
    ones_two = jnp.where(iota((256, 128), 1) < 2, 1.0, 0.0).astype(BF)
    use_q = jnp.concatenate([usable, usable], axis=1)
    for p in range(N):
        qx[128:256, p * 128 : p * 128 + 128] = query_mask
        keys[p * 128 : p * 128 + 128, 128:256] = key_mask
    vals_t[128:144, :] = jnp.ones((16, 2048), BF)
    gx[128:256, :] = jnp.zeros((128, 2048), BF)

    chip = lax.div(row, 2)

    def place(i):
        return block_of(lax.rem(i, 2) * 4 + lax.div(i, 2), 256)

    def prepare(chip, i):
        at, qat = block_of(chip, 256), place(i)
        piece = tokens[:, at].astype(F32)
        tile = jnp.concatenate([piece, piece], axis=0).T.astype(BF)
        qkv = nn(tile, ew[...])
        x = qkv[:, 0:128]
        xq[qat, :] = x
        r = lax.rsqrt(jnp.mean(x * x, axis=1, keepdims=True) + EPS)
        rq[qat, :] = jnp.broadcast_to(r, (256, 128))
        query = x * (r * (scale / LN2)) * gain_q
        q_n[qat, :] = query.astype(BF)
        qx[0:128, qat] = query.T.astype(BF)
        x = qkv[:, 128:256]
        xk[at, :] = x
        r = lax.rsqrt(jnp.mean(x * x, axis=1, keepdims=True) + EPS)
        rk[at, :] = jnp.broadcast_to(r, (256, 128))
        key = x * r * gain_k
        keys[at, 0:128] = key.astype(BF)
        keys_t[:, at] = key.T.astype(BF)
        val = qkv[:, 256:384]
        vals[at, 0:128] = val.astype(BF)
        vals[at, 128:256] = ones_two
        vals_t[0:128, at] = val.T.astype(BF)

    def near(i):
        half = lax.div(i, 2)
        return jnp.where(lax.rem(i, 2) == 1, half + 1, 8 - half)

    def pass_on(i):
        to_chip(near(i)).wait_recv()
        to_other(near(i)).start()

    to_other(0).wait_recv()
    prepare(chip, 0)
    pass_on(1)

    def arrive(i, _):
        pass_on(i + 1)
        to_other(near(i)).wait_recv()
        prepare(lax.rem(chip + 8 - near(i), 8), lax.rem(8 - near(i), 8))
        return 0

    lax.fori_loop(1, 7, arrive, 0)
    to_other(4).wait_recv()
    prepare(lax.rem(chip + 4, 8), 4)

    def sent(k, _):
        to_chip(k).wait_send()
        to_other(k).wait_send()
        return 0

    lax.fori_loop(1, 8, sent, 0)
    to_other(0).wait_send()

    def send_out(p):
        return remote(outs.at[block_of(p)], att.at[:, block_of(row)], att_send.at[p], att_recv.at[row], seq=p)

    own_out = pltpu.make_async_copy(outs.at[block_of(row)], att.at[:, block_of(row)], own_sem.at[1])

    def score(i, buffer, c):
        kc = pl.ds(c * 512, 512)
        buffer[kc, block_of(lax.div(i, 2), 256)] = jnp.exp2(nn(keys[kc, :], qx[:, place(i)])).astype(BF)

    def output(i, buffer, c):
        kc = pl.ds(c * 512, 512)
        return nn(vals_t[:, kc], buffer[kc, block_of(lax.div(i, 2), 256)])

    def finish(i, out):
        at = place(i)
        inverse = 1.0 / out[128:129, :]
        out = out[0:128, :] * inverse
        inv[0:1, at] = inverse
        out_t[:, at] = out
        qb = lax.rem(chip + i, 8)
        outs[block_of(qb, 256), :] = (out * use_q).T.astype(BF)
        for p in (qb * 2, qb * 2 + 1):

            @pl.when(p != row)
            def _():
                send_out(p).start()

            @pl.when(p == row)
            def _():
                own_out.start()

    def pair(i, buffer, following):
        out = jnp.zeros((144, 256), F32)
        for c in range(4):
            score(i + 1, following, c)
            out = out + output(i, buffer, c)
        finish(i, out)

    for c in range(4):
        score(0, even, c)

    def forward(j, _):
        pair(2 * j, even, odd)
        pair(2 * j + 1, odd, even)
        return 0

    lax.fori_loop(0, 3, forward, 0)
    pair(6, even, odd)
    finish(7, nn(vals_t[...], odd[:, 768:1024]))

    def cot_wait(k, _):
        cot_copy(k).wait()
        return 0

    lax.fori_loop(1, N, cot_wait, 0)
    own_cot.wait()

    def incoming_rows(i, _):
        at = place(i)
        up = jnp.where(use_q > 0.0, incoming[block_of(lax.rem(chip + i, 8), 256), :].astype(F32).T, 0.0)
        up = (up * inv[0:1, at]).astype(BF)
        wide = up.astype(F32)
        delta = jnp.sum(wide * out_t[:, at], axis=0, keepdims=True)
        high, low = split(-delta)
        line = iota((16, 256), 0)
        extra = jnp.where(line == 0, high.astype(F32), jnp.where(line == 1, low.astype(F32), 0.0))
        gx[0:128, at] = up
        gx[128:144, at] = extra.astype(BF)
        up_n[at, :] = wide.T.astype(BF)
        return 0

    lax.fori_loop(0, 8, incoming_rows, 0)

    def rms_back(x, r, gain, grad):
        scaled = gain * grad
        mean = jnp.mean(x * scaled, axis=1, keepdims=True)
        return (r * (scaled - x * (r * r * mean))).astype(BF)

    def score_back(i, _):
        at = block_of(i, 1024)
        for c in range(4):
            qc = pl.ds(c * 512, 512)
            e = (even, odd)[c // 2][at, c % 2 * 512 : c % 2 * 512 + 512]
            dss[at, qc] = (e.astype(F32) * nn(vals[at, :], gx[:, qc])).astype(BF)
        return 0

    def query_back(i, total):
        at = block_of(i, 1024)
        grad = nn(keys_t[...], dss[:, at]).T * scale
        x, r = xq[at, :], rq[at, :]
        back = rms_back(x, r, gain_q, grad)
        for n in range(1024 // 256):
            place_n = i * 4 + n
            block = lax.rem(place_n, 4) * 2 + lax.div(place_n, 4)
            dxq[block_of(lax.rem(chip + block, 8), 256), :] = back[n * 256 : n * 256 + 256, :]
        return total + jnp.sum(grad * x * r, axis=0, keepdims=True)

    def value_back(i, _):
        at = block_of(i, 1024)
        dvs[at, :] = (nn(even[at, :], up_n[0:1024, :]) + nn(odd[at, :], up_n[1024:2048, :])).astype(BF)
        return 0

    def key_back(i, _):
        at = block_of(i, 1024)
        dks[at, :] = rms_back(xk[at, :], rk[at, :], gain_k, nn(dss[at, :], q_n[...]) * LN2)
        return 0

    def share(j, grads, send, recv):
        parts[j, slab] = nn(tokens[...], grads[...]).astype(BF)
        mine = parts.at[j, slab]
        return to_all(lambda k: remote(mine, mine, send.at[k], recv.at[k], dp=peer("dp", k)))

    lax.fori_loop(0, 2, score_back, 0)
    norm_q = lax.fori_loop(0, 2, query_back, jnp.zeros((1, 128), F32))
    line = iota((8, 128), 0)
    norms[row] = jnp.where(line == 0, norm_q, jnp.where(line == 1, norm_q * gain_q / gain_k, 0.0))
    norm_wait = to_all(
        lambda k: remote(norms.at[row], norms.at[row], nrm_send.at[k], nrm_recv.at[k], seq=peer("seq", k))
    )
    q_wait = share(0, dxq, q_send, q_recv)
    lax.fori_loop(0, 2, value_back, 0)
    v_wait = share(2, dvs, v_send, v_recv)
    lax.fori_loop(0, 2, key_back, 0)
    k_wait = share(1, dks, k_send, k_recv)
    norm_wait()
    norm = norms[0]
    for j in range(1, N):
        norm = norm + norms[j]
    sums[slab] = norm
    ag_wait = to_all(
        lambda k: remote(sums.at[slab], sums.at[slab], ag_send.at[k], ag_recv.at[k], dp=peer("dp", k))
    )
    columns = embed[:, block_of(slab)].astype(F32).T.astype(BF)

    def project(j):
        whole_sum = parts[j, 0].astype(F32)
        for i in range(1, N):
            whole_sum = whole_sum + parts[j, i].astype(F32)
        high, low = split(whole_sum)
        proj_out[pl.ds(j, 128, stride=3), :] = nn(columns, high) + nn(columns, low)

    def out_wait(p, _):
        @pl.when(p != row)
        def _():
            send_out(p).wait_send()
            remote(outs.at[block_of(p)], att.at[:, block_of(p)], att_send.at[p], att_recv.at[p], seq=p).wait_recv()

        return 0

    lax.fori_loop(0, N, out_wait, 0)
    own_out.wait()
    q_wait()
    project(0)
    v_wait()
    project(2)
    k_wait()
    project(1)
    ag_wait()
    norm = sums[0]
    for j in range(1, N):
        norm = norm + sums[j]
    norm_out[...] = norm[0:2, :]


def body(
    features,
    conv_weight,
    clip_frames,
    clip_group,
    clip_offset,
    clip_times,
    noise_tokens,
    embed_weight,
    attention_proj,
    norm_gains,
    cotangent,
):
    dma = pltpu.SemaphoreType.DMA
    vm = pltpu.VMEM
    in_hbm = lambda x: pltpu.with_memory_space_constraint(x, pltpu.HBM)
    noisy, att, grads, norms = pl.pallas_call(
        whole,
        name="whole",
        out_shape=(vm((64, 128), F32), vm((128, 2048), BF), vm((384, 128), F32), vm((2, 128), F32)),
        in_specs=[pl.BlockSpec(memory_space=pltpu.HBM)] * 11,
        out_specs=[pl.BlockSpec(memory_space=vm)] * 4,
        scratch_shapes=[
            vm((512, 512), BF), vm((432, 512), BF), vm((3, 1, 32), jnp.int32), vm((1, 32), F32), vm((64, 128), BF),
            vm((64, 2048), BF), vm((3, 2048, 128), BF), vm((2, 128), F32),
            vm((8, 128), F32), vm((4, 512, 128), F32), vm((512, 512), BF), vm((432, 512), F32),
            vm((2, 32, 128), F32), vm((2, 32, 128), F32), vm((64, 128), F32),
            vm((2, 32, 128), F32), vm((2, 32, 128), F32), vm((1, 64, 128), F32), vm((64, 2048), BF),
            vm((64, 2048), BF), vm((2048, 128), BF), vm((128, 384), BF),
            vm((2048, 256), BF), vm((2048, 256), BF), vm((128, 2048), BF), vm((144, 2048), BF),
            vm((2048, 128), F32), vm((2048, 128), F32), vm((2048, 128), F32), vm((2048, 128), F32), vm((256, 2048), BF), vm((256, 2048), BF),
            vm((2048, 128), BF), vm((2048, 128), BF), vm((128, 2048), F32), vm((8, 2048), F32),
            vm((2048, 1024), BF), vm((2048, 1024), BF), vm((2048, 2048), BF), vm((2048, 128), BF), vm((2048, 128), BF), vm((2048, 128), BF), vm((2048, 128), BF),
            vm((3, N, 64, 128), BF), vm((N, 8, 128), F32), vm((N, 8, 128), F32),
            dma((10,)), dma((5,)), dma((5,)), dma((N,)), dma((N,)), dma((8,)), dma((8,)), dma((8,)), dma((8,)),
            dma((N,)), dma((N,)), dma((2,)), dma((N,)), dma((N,)), dma((N,)), dma((N,)), dma((N,)), dma((N,)),
            dma((N,)), dma((N,)), dma((N,)), dma((N,)), dma((N,)), dma((N,)),
        ],
        compiler_params=pltpu.CompilerParams(collective_id=0, has_side_effects=True, vmem_limit_bytes=48 * 2**20),
    )(
        in_hbm(features.reshape(512, 512)),
        in_hbm(conv_weight.reshape(432, 512)),
        in_hbm(clip_frames.reshape(1, 32)),
        in_hbm(clip_group.reshape(1, 32)),
        in_hbm(clip_offset.reshape(1, 32)),
        in_hbm(clip_times.reshape(1, 32)),
        in_hbm(noise_tokens.transpose(0, 2, 1).reshape(64, 128)),
        in_hbm(embed_weight),
        in_hbm(attention_proj.transpose(1, 2, 0, 3).reshape(3, 2048, 128)),
        in_hbm(norm_gains),
        in_hbm(cotangent.reshape(128, 2048)),
    )
    return (
        noisy.reshape(1, 64, 128).transpose(0, 2, 1),
        att.reshape(1, 128, 2048),
        grads.reshape(128, 3, 1, 128),
        norms,
    )


def solution(mesh):
    return jax.shard_map(
        body,
        mesh=mesh,
        in_specs=(
            P("dp", "seq", None, None),
            P(),
            P(),
            P(),
            P(),
            P(),
            P("dp", "seq", None),
            P(),
            P(None, None, "seq", None),
            P(),
            P("dp", "seq", None),
        ),
        out_specs=(P("dp", "seq", None), P("dp", "seq", None), P("dp", None, "seq", None), P()),
        check_vma=False,
    )
```

```python
import jax
import jax.numpy as jnp
from jax import lax
from jax.experimental import pallas as pl
from jax.experimental.pallas import tpu as pltpu
from jax.sharding import PartitionSpec as P

F32 = jnp.float32
BF = jnp.bfloat16
N = 16
LN2 = 0.6931471805599453
MASKED = -300.0
EPS = 1e-06


def nn(a, b):
    return lax.dot_general(a, b, (((1,), (0,)), ((), ())), preferred_element_type=F32)


def nt(a, b):
    return lax.dot_general(a, b, (((1,), (1,)), ((), ())), preferred_element_type=F32)


def iota(shape, dim):
    return lax.broadcasted_iota(jnp.int32, shape, dim)


def block_of(i, size=128):
    return pl.ds(pl.multiple_of(i * size, size), size)


def peer(axis, k):
    return lax.rem(lax.axis_index(axis) + k + N, N)


def greet():
    barrier = pltpu.get_barrier_semaphore()

    def signal(**where):
        pl.semaphore_signal(barrier, inc=1, device_id=where, device_id_type=pl.DeviceIdType.MESH)

    def both(k, _):
        signal(dp=peer("dp", k))
        signal(seq=peer("seq", k))
        return 0

    lax.fori_loop(1, N, both, 0)
    for a in (-1, 1):
        for b in (-1, 1):
            signal(dp=peer("dp", a), seq=peer("seq", b))
    return lambda: pl.semaphore_wait(barrier, 2 * (N - 1) + 4)


def remote(src, dst, send, recv, **where):
    return pltpu.make_async_remote_copy(
        src_ref=src,
        dst_ref=dst,
        send_sem=send,
        recv_sem=recv,
        device_id=where,
        device_id_type=pl.DeviceIdType.MESH,
    )


def to_all(make):
    def start(k, _):
        make(k).start()
        return 0

    def wait(k, _):
        make(k).wait()
        return 0

    lax.fori_loop(1, N, start, 0)
    return lambda: lax.fori_loop(1, N, wait, 0)


def split(x):
    high = x.astype(BF)
    return high, (x - high.astype(F32)).astype(BF)


def whole(
    feat_h, wconv_h, frames_h, group_h, offset_h, times_h, noise_h, embed_h, proj_h, gains_h, cot,
    noisy, att, proj_out, norm_out,
    feat, wconv, ints, times_v, noise, embed, proj, gains,
    tab, actf, actp, conv, edge_out, late_out, own_late, edge_in, late_in, own_late_in, gath,
    tokens, incoming, ew, keys, vals, keys_t, vals_t, xq, xk, rq, rk, qx, gx, q_n, up_n, out_t, inv, even, odd, dss, dxq, dks, dvs, outs,
    parts, sums, norms,
    in_sem, edge_send, edge_recv, dp_send, dp_recv, z_send, z_recv, sib_send, sib_recv,
    cot_send, cot_recv, own_sem, att_send, att_recv, q_send, q_recv, k_send, k_recv, v_send, v_recv,
    nrm_send, nrm_recv, ag_send, ag_recv,
):
    slab = lax.axis_index("dp")
    row = lax.axis_index("seq")
    other = row + 1 - 2 * lax.rem(row, 2)
    fetches = []
    for src, dst in (
        (feat_h, feat), (wconv_h, wconv), (frames_h, ints.at[0]), (group_h, ints.at[1]), (offset_h, ints.at[2]),
        (times_h, times_v), (embed_h, embed), (proj_h, proj), (noise_h, noise), (gains_h, gains),
    ):
        fetches.append(pltpu.make_async_copy(src, dst, in_sem.at[len(fetches)]))
        fetches[-1].start()
    entered = greet()
    fetches[0].wait()
    for q in range(4):
        x = feat[:, q * 128 : q * 128 + 128].astype(F32)
        actf[q] = x / (1.0 + jnp.exp(-x))

    for part in range(4):
        r, b = part // 2, part % 2
        for t in range(8):
            for q in range(4):
                rows = actf[q, pl.ds(t * 64 + r * 32 + b, 16, stride=2), :]
                actp[pl.ds((part * 8 + t) * 16, 16), q * 128 : q * 128 + 128] = rows.astype(BF)
    fetches[1].wait()
    conv[...] = nt(wconv[...], actp[...])

    for i in range(2, 6):
        fetches[i].wait()
    tab[...] = jnp.zeros((8, 128), F32)
    for i in range(3):
        tab[i : i + 1, 0:32] = ints[i].astype(F32)
    tab[3:4, 0:32] = times_v[...]
    by_clip = tab[...].T
    frames, group, offset, times = [by_clip[0:32, i : i + 1] for i in range(4)]
    earlier = iota((32, 128), 1) < iota((32, 128), 0)
    starts = jnp.sum(jnp.where(earlier, tab[0:1, :], 0.0), axis=1, keepdims=True)
    lane = iota((1, 128), 1)
    slot_i = lax.shift_right_logical(lane, 4)
    col_i = lax.bitwise_and(lane, 15)
    slot = slot_i.astype(F32)
    in_slot = (group == slab.astype(F32)) & (slot >= offset) & (slot < offset + frames)
    over_clips = lambda v: jnp.sum(jnp.where(in_slot, v, 0.0), axis=0, keepdims=True)
    number = iota((32, 128), 0).astype(F32)
    usable = over_clips(1.0 + 0.0 * number)
    usable = jnp.where(usable > 0.0, 1.0, 0.0)
    segment = over_clips(number + 1.0) - 1.0
    source = over_clips(starts + slot - offset)
    level = over_clips(times + 0.0 * number)

    def own_start(frame):
        inside = (starts <= frame) & (frame < starts + frames)
        return jnp.sum(jnp.where(inside, starts, 0.0), axis=0, keepdims=True)

    here = slab.astype(F32) * 8.0 + slot
    after = here + 8.0
    start_here, start_after = own_start(here), own_start(after)
    keep = []
    for dt in range(3):
        main = (here - dt >= start_here) & (slot_i >= dt)
        late = (after - dt >= start_after) & (slot_i < dt)
        keep.append((jnp.where(main, 1.0, 0.0), jnp.where(late, 1.0, 0.0)))

    not_first = jnp.where(col_i > 0, 1.0, 0.0)
    not_last = jnp.where(col_i < 15, 1.0, 0.0)

    def tap(dt, dr, dw, r, ob):
        at = (((2 - dt) * 3 + dr + 1) * 3 + dw + 1) * 16
        b = (ob + dw) % 2
        piece = conv[at : at + 16, (r * 2 + b) * 128 : (r * 2 + b) * 128 + 128]
        if ob + dw == -1:
            return pltpu.roll(piece, 1, 1) * not_first
        if ob + dw == 2:
            return pltpu.roll(piece, 127, 1) * not_last
        return piece

    def sums_of(out_row, ob):
        main = late = None
        for dt in range(3):
            total = None
            for r in range(2):
                dr = r - out_row
                if abs(dr) <= 1:
                    for dw in range(-1, 2):
                        term = tap(dt, dr, dw, r, ob)
                        total = term if total is None else total + term
            if dt:
                total = pltpu.roll(total, 16 * dt, 1)
            m = total * keep[dt][0]
            main = m if main is None else main + m
            if dt:
                m = total * keep[dt][1]
                late = m if late is None else late + m
        return main, late

    for side, out_row in ((0, -1), (1, 2)):
        for ob in range(2):
            at = slice(ob * 16, ob * 16 + 16)
            edge_out[side, at, :], late_out[side, at, :] = sums_of(out_row, ob)
    entered()

    routes = []
    for side, step in ((0, -1), (1, 1)):
        goes = (row > 0) if side == 0 else (row < N - 1)
        comes = (row < N - 1) if side == 0 else (row > 0)
        routes.append((
            remote(edge_out.at[side], edge_in.at[1 - side], edge_send.at[side], edge_recv.at[side], seq=peer("seq", step)),
            goes, comes, edge_in, 1 - side,
        ))
        routes.append((
            remote(
                late_out.at[side], late_in.at[1 - side], edge_send.at[2 + side], edge_recv.at[2 + side],
                dp=peer("dp", 1), seq=peer("seq", step),
            ),
            goes & (slab < N - 1), comes & (slab > 0), late_in, 1 - side,
        ))
    routes.append((
        remote(own_late, own_late_in.at[0], edge_send.at[4], edge_recv.at[4], dp=peer("dp", 1)),
        slab < N - 1, slab > 0, own_late_in, 0,
    ))
    for copy, goes, _, _, _ in routes[:4]:
        pl.when(goes)(copy.start)
    mains = {}
    for a in range(2):
        for ob in range(2):
            at = slice((a * 2 + ob) * 16, (a * 2 + ob) * 16 + 16)
            mains[a, ob], own_late[at, :] = sums_of(a, ob)
    pl.when(routes[4][1])(routes[4][0].start)
    def cot_copy(k):
        return remote(
            cot.at[:, block_of(peer("seq", k))], incoming.at[block_of(row)], cot_send.at[k], cot_recv.at[k],
            seq=peer("seq", k),
        )

    own_cot = pltpu.make_async_copy(cot.at[:, block_of(row)], incoming.at[block_of(row)], own_sem.at[0])
    own_cot.start()
    for _, _, comes, dst, i in routes:

        @pl.when(jnp.logical_not(comes))
        def _():
            dst[i] = jnp.zeros(dst.shape[1:], F32)

    fetches[6].wait()
    fetches[7].wait()
    for j in range(3):
        high, low = split(nn(embed[...], proj[j]))
        ew[0:64, j * 128 : j * 128 + 128] = high
        ew[64:128, j * 128 : j * 128 + 128] = low
    base = source * 16.0 + col_i.astype(F32)
    select = jnp.where(iota((2048, 128), 0).astype(F32) == base, 1.0, 0.0).astype(BF)
    fetches[8].wait()
    fetches[9].wait()

    for copy, goes, comes, _, _ in routes:
        pl.when(goes)(copy.wait_send)
        pl.when(comes)(copy.wait_recv)
    for a in range(2):
        for ob in range(2):
            at = slice((a * 2 + ob) * 16, (a * 2 + ob) * 16 + 16)
            side = slice(ob * 16, ob * 16 + 16)
            total = mains[a, ob] + edge_in[a, side, :] + late_in[a, side, :] + own_late_in[0, at, :]
            gath[at, block_of(slab)] = total.astype(BF)
    mine = gath.at[:, block_of(slab)]
    gath_wait = to_all(lambda k: remote(mine, mine, dp_send.at[k], dp_recv.at[k], dp=peer("dp", k)))

    for k in (1, 15, 2, 14, 3, 13):
        cot_copy(k).start()
    gath_wait()

    made = usable * ((1.0 - level) * nn(gath[...], select) + level * noise[...].astype(F32))
    noisy[...] = made
    tokens[:, block_of(row)] = made.astype(BF)

    def tile_of(k):
        return tokens.at[:, block_of(peer("seq", -2 * k))]

    def to_chip(k):
        return remote(tile_of(0), tile_of(0), z_send.at[k], z_recv.at[k], seq=peer("seq", 2 * k))

    def to_other(k):
        return remote(tile_of(k), tile_of(k), sib_send.at[k], sib_recv.at[k], seq=other)

    for k in (4, 3, 5, 2, 6, 1, 7):
        to_chip(k).start()
    to_other(0).start()
    for k in (4, 12, 5, 11, 6, 10, 7, 9, 8):
        cot_copy(k).start()

    scale = 128.0**-0.5
    gain_q, gain_k = gains[0:1, :], gains[1:2, :]
    by_lane = jnp.broadcast_to(segment, (128, 128))
    by_row = by_lane.T
    key_mask = jnp.where(iota((128, 128), 1).astype(F32) - 1.0 == by_row, 0.0, MASKED).astype(BF)
    query_mask = jnp.where(iota((128, 128), 0).astype(F32) - 1.0 == by_lane, 1.0, 0.0).astype(BF)
    ones_two = jnp.where(iota((256, 128), 1) < 2, 1.0, 0.0).astype(BF)
    use_q = jnp.concatenate([usable, usable], axis=1)
    for p in range(N):
        qx[128:256, p * 128 : p * 128 + 128] = query_mask
        keys[p * 128 : p * 128 + 128, 128:256] = key_mask
    vals_t[128:144, :] = jnp.ones((16, 2048), BF)
    gx[128:256, :] = jnp.zeros((128, 2048), BF)

    chip = lax.div(row, 2)

    def place(i):
        return block_of(lax.rem(i, 2) * 4 + lax.div(i, 2), 256)

    def prepare(chip, i):
        at, qat = block_of(chip, 256), place(i)
        piece = tokens[:, at].astype(F32)
        tile = jnp.concatenate([piece, piece], axis=0).T.astype(BF)
        qkv = nn(tile, ew[...])
        x = qkv[:, 0:128]
        xq[qat, :] = x
        r = lax.rsqrt(jnp.mean(x * x, axis=1, keepdims=True) + EPS)
        rq[qat, :] = jnp.broadcast_to(r, (256, 128))
        query = x * (r * (scale / LN2)) * gain_q
        q_n[qat, :] = query.astype(BF)
        qx[0:128, qat] = query.T.astype(BF)
        x = qkv[:, 128:256]
        xk[at, :] = x
        r = lax.rsqrt(jnp.mean(x * x, axis=1, keepdims=True) + EPS)
        rk[at, :] = jnp.broadcast_to(r, (256, 128))
        key = x * r * gain_k
        keys[at, 0:128] = key.astype(BF)
        keys_t[:, at] = key.T.astype(BF)
        val = qkv[:, 256:384]
        vals[at, 0:128] = val.astype(BF)
        vals[at, 128:256] = ones_two
        vals_t[0:128, at] = val.T.astype(BF)

    def near(i):
        half = lax.div(i, 2)
        return jnp.where(lax.rem(i, 2) == 1, half + 1, 8 - half)

    def pass_on(i):
        to_chip(near(i)).wait_recv()
        to_other(near(i)).start()

    to_other(0).wait_recv()
    prepare(chip, 0)
    pass_on(1)

    def arrive(i, _):
        pass_on(i + 1)
        to_other(near(i)).wait_recv()
        prepare(lax.rem(chip + 8 - near(i), 8), lax.rem(8 - near(i), 8))
        return 0

    lax.fori_loop(1, 7, arrive, 0)
    to_other(4).wait_recv()
    prepare(lax.rem(chip + 4, 8), 4)

    def sent(k, _):
        to_chip(k).wait_send()
        to_other(k).wait_send()
        return 0

    lax.fori_loop(1, 8, sent, 0)
    to_other(0).wait_send()

    def send_out(p):
        return remote(outs.at[block_of(p)], att.at[:, block_of(row)], att_send.at[p], att_recv.at[row], seq=p)

    own_out = pltpu.make_async_copy(outs.at[block_of(row)], att.at[:, block_of(row)], own_sem.at[1])

    def score(i, buffer, c):
        kc = pl.ds(c * 512, 512)
        buffer[kc, block_of(lax.div(i, 2), 256)] = jnp.exp2(nn(keys[kc, :], qx[:, place(i)])).astype(BF)

    def output(i, buffer, c):
        kc = pl.ds(c * 512, 512)
        return nn(vals_t[:, kc], buffer[kc, block_of(lax.div(i, 2), 256)])

    def finish(i, out):
        at = place(i)
        inverse = 1.0 / out[128:129, :]
        out = out[0:128, :] * inverse
        inv[0:1, at] = inverse
        out_t[:, at] = out
        qb = lax.rem(chip + i, 8)
        outs[block_of(qb, 256), :] = (out * use_q).T.astype(BF)
        for p in (qb * 2, qb * 2 + 1):

            @pl.when(p != row)
            def _():
                send_out(p).start()

            @pl.when(p == row)
            def _():
                own_out.start()

    def pair(i, buffer, following):
        out = jnp.zeros((144, 256), F32)
        for c in range(4):
            score(i + 1, following, c)
            out = out + output(i, buffer, c)
        finish(i, out)

    for c in range(4):
        score(0, even, c)

    def forward(j, _):
        pair(2 * j, even, odd)
        pair(2 * j + 1, odd, even)
        return 0

    lax.fori_loop(0, 3, forward, 0)
    pair(6, even, odd)
    finish(7, nn(vals_t[...], odd[:, 768:1024]))

    def cot_wait(k, _):
        cot_copy(k).wait()
        return 0

    lax.fori_loop(1, N, cot_wait, 0)
    own_cot.wait()

    def incoming_rows(i, _):
        at = place(i)
        up = jnp.where(use_q > 0.0, incoming[block_of(lax.rem(chip + i, 8), 256), :].astype(F32).T, 0.0)
        up = (up * inv[0:1, at]).astype(BF)
        wide = up.astype(F32)
        delta = jnp.sum(wide * out_t[:, at], axis=0, keepdims=True)
        high, low = split(-delta)
        line = iota((16, 256), 0)
        extra = jnp.where(line == 0, high.astype(F32), jnp.where(line == 1, low.astype(F32), 0.0))
        gx[0:128, at] = up
        gx[128:144, at] = extra.astype(BF)
        up_n[at, :] = wide.T.astype(BF)
        return 0

    lax.fori_loop(0, 8, incoming_rows, 0)

    def rms_back(x, r, gain, grad):
        scaled = gain * grad
        mean = jnp.mean(x * scaled, axis=1, keepdims=True)
        return (r * (scaled - x * (r * r * mean))).astype(BF)

    def score_back(i, _):
        at = block_of(i, 1024)
        for c in range(4):
            qc = pl.ds(c * 512, 512)
            e = (even, odd)[c // 2][at, c % 2 * 512 : c % 2 * 512 + 512]
            dss[at, qc] = (e.astype(F32) * nn(vals[at, :], gx[:, qc])).astype(BF)
        return 0

    def query_back(i, total):
        at = block_of(i, 1024)
        grad = nn(keys_t[...], dss[:, at]).T * scale
        x, r = xq[at, :], rq[at, :]
        back = rms_back(x, r, gain_q, grad)
        for n in range(1024 // 256):
            place_n = i * 4 + n
            block = lax.rem(place_n, 4) * 2 + lax.div(place_n, 4)
            dxq[block_of(lax.rem(chip + block, 8), 256), :] = back[n * 256 : n * 256 + 256, :]
        return total + jnp.sum(grad * x * r, axis=0, keepdims=True)

    def value_back(i, _):
        at = block_of(i, 1024)
        dvs[at, :] = (nn(even[at, :], up_n[0:1024, :]) + nn(odd[at, :], up_n[1024:2048, :])).astype(BF)
        return 0

    def key_back(i, _):
        at = block_of(i, 1024)
        dks[at, :] = rms_back(xk[at, :], rk[at, :], gain_k, nn(dss[at, :], q_n[...]) * LN2)
        return 0

    def share(j, grads, send, recv):
        parts[j, slab] = nn(tokens[...], grads[...]).astype(BF)
        mine = parts.at[j, slab]
        return to_all(lambda k: remote(mine, mine, send.at[k], recv.at[k], dp=peer("dp", k)))

    lax.fori_loop(0, 2, score_back, 0)
    norm_q = lax.fori_loop(0, 2, query_back, jnp.zeros((1, 128), F32))
    line = iota((8, 128), 0)
    norms[row] = jnp.where(line == 0, norm_q, jnp.where(line == 1, norm_q * gain_q / gain_k, 0.0))
    norm_wait = to_all(
        lambda k: remote(norms.at[row], norms.at[row], nrm_send.at[k], nrm_recv.at[k], seq=peer("seq", k))
    )
    q_wait = share(0, dxq, q_send, q_recv)
    lax.fori_loop(0, 2, value_back, 0)
    v_wait = share(2, dvs, v_send, v_recv)
    lax.fori_loop(0, 2, key_back, 0)
    k_wait = share(1, dks, k_send, k_recv)
    norm_wait()
    norm = norms[0]
    for j in range(1, N):
        norm = norm + norms[j]
    sums[slab] = norm
    ag_wait = to_all(
        lambda k: remote(sums.at[slab], sums.at[slab], ag_send.at[k], ag_recv.at[k], dp=peer("dp", k))
    )
    columns = embed[:, block_of(slab)].astype(F32).T.astype(BF)

    def project(j):
        whole_sum = parts[j, 0].astype(F32)
        for i in range(1, N):
            whole_sum = whole_sum + parts[j, i].astype(F32)
        high, low = split(whole_sum)
        proj_out[pl.ds(j, 128, stride=3), :] = nn(columns, high) + nn(columns, low)

    def out_wait(p, _):
        @pl.when(p != row)
        def _():
            send_out(p).wait_send()
            remote(outs.at[block_of(p)], att.at[:, block_of(p)], att_send.at[p], att_recv.at[p], seq=p).wait_recv()

        return 0

    lax.fori_loop(0, N, out_wait, 0)
    own_out.wait()
    q_wait()
    project(0)
    v_wait()
    project(2)
    k_wait()
    project(1)
    ag_wait()
    norm = sums[0]
    for j in range(1, N):
        norm = norm + sums[j]
    norm_out[...] = norm[0:2, :]


def body(
    features,
    conv_weight,
    clip_frames,
    clip_group,
    clip_offset,
    clip_times,
    noise_tokens,
    embed_weight,
    attention_proj,
    norm_gains,
    cotangent,
):
    dma = pltpu.SemaphoreType.DMA
    vm = pltpu.VMEM
    in_hbm = lambda x: pltpu.with_memory_space_constraint(x, pltpu.HBM)
    noisy, att, grads, norms = pl.pallas_call(
        whole,
        name="whole",
        out_shape=(vm((64, 128), F32), vm((128, 2048), BF), vm((384, 128), F32), vm((2, 128), F32)),
        in_specs=[pl.BlockSpec(memory_space=pltpu.HBM)] * 11,
        out_specs=[pl.BlockSpec(memory_space=vm)] * 4,
        scratch_shapes=[
            vm((512, 512), BF), vm((432, 512), BF), vm((3, 1, 32), jnp.int32), vm((1, 32), F32), vm((64, 128), BF),
            vm((64, 2048), BF), vm((3, 2048, 128), BF), vm((2, 128), F32),
            vm((8, 128), F32), vm((4, 512, 128), F32), vm((512, 512), BF), vm((432, 512), F32),
            vm((2, 32, 128), F32), vm((2, 32, 128), F32), vm((64, 128), F32),
            vm((2, 32, 128), F32), vm((2, 32, 128), F32), vm((1, 64, 128), F32), vm((64, 2048), BF),
            vm((64, 2048), BF), vm((2048, 128), BF), vm((128, 384), BF),
            vm((2048, 256), BF), vm((2048, 256), BF), vm((128, 2048), BF), vm((144, 2048), BF),
            vm((2048, 128), F32), vm((2048, 128), F32), vm((2048, 128), F32), vm((2048, 128), F32), vm((256, 2048), BF), vm((256, 2048), BF),
            vm((2048, 128), BF), vm((2048, 128), BF), vm((128, 2048), F32), vm((8, 2048), F32),
            vm((2048, 1024), BF), vm((2048, 1024), BF), vm((2048, 2048), BF), vm((2048, 128), BF), vm((2048, 128), BF), vm((2048, 128), BF), vm((2048, 128), BF),
            vm((3, N, 64, 128), BF), vm((N, 8, 128), F32), vm((N, 8, 128), F32),
            dma((10,)), dma((5,)), dma((5,)), dma((N,)), dma((N,)), dma((8,)), dma((8,)), dma((8,)), dma((8,)),
            dma((N,)), dma((N,)), dma((2,)), dma((N,)), dma((N,)), dma((N,)), dma((N,)), dma((N,)), dma((N,)),
            dma((N,)), dma((N,)), dma((N,)), dma((N,)), dma((N,)), dma((N,)),
        ],
        compiler_params=pltpu.CompilerParams(collective_id=0, has_side_effects=True, vmem_limit_bytes=48 * 2**20),
    )(
        in_hbm(features.reshape(512, 512)),
        in_hbm(conv_weight.reshape(432, 512)),
        in_hbm(clip_frames.reshape(1, 32)),
        in_hbm(clip_group.reshape(1, 32)),
        in_hbm(clip_offset.reshape(1, 32)),
        in_hbm(clip_times.reshape(1, 32)),
        in_hbm(noise_tokens.transpose(0, 2, 1).reshape(64, 128)),
        in_hbm(embed_weight),
        in_hbm(attention_proj.transpose(1, 2, 0, 3).reshape(3, 2048, 128)),
        in_hbm(norm_gains),
        in_hbm(cotangent.reshape(128, 2048)),
    )
    return (
        noisy.reshape(1, 64, 128).transpose(0, 2, 1),
        att.reshape(1, 128, 2048),
        grads.reshape(128, 3, 1, 128),
        norms,
    )


def solution(mesh):
    return jax.shard_map(
        body,
        mesh=mesh,
        in_specs=(
            P("dp", "seq", None, None),
            P(),
            P(),
            P(),
            P(),
            P(),
            P("dp", "seq", None),
            P(),
            P(None, None, "seq", None),
            P(),
            P("dp", "seq", None),
        ),
        out_specs=(P("dp", "seq", None), P("dp", "seq", None), P("dp", None, "seq", None), P()),
        check_vma=False,
    )
```
